128 devices in a mesh: gx: 4 (over y_lo, core), gy: 8 (over y_hi, x), gz: 4 (over z).
Axes of the slice: x: 4, y: 4 (y_hi: 2, y_lo: 2; y = y_hi * 2 + y_lo), z: 4, core: 2. Of those that a mesh axis runs over, the one named last changes fastest.
Arguments:
- species: int32 [16384], P(('gx', 'gy', 'gz')), may hold values from 0 to 7
- send_list: int32 [8, 16, 8, 4], P('gx', 'gy', 'gz'), may hold values from 0 to 127, as said below
- neighbours: int32 [16, 16384], P(None, ('gx', 'gy', 'gz')), may hold values from 0 to 383, as said below
- edge_vectors: float32 [3, 16, 16384], P(None, None, ('gx', 'gy', 'gz')), may hold values from -6 to 6, as said below
- embedding: bfloat16 [8, 128], replicated, may hold values from -6 to 6
- radial_in: float32 [2, 8, 64], replicated, may hold values from -3 to 3
- radial_mid: float32 [2, 64, 64], replicated, may hold values from -1 to 1
- radial_out: float32 [2, 64, 384], replicated, may hold values from -1.5 to 1.5
- mixing: float32 [2, 384, 128], replicated, may hold values from -0.3125 to 0.3125
- read_linear: float32 [128], replicated, may hold values from -0.5 to 0.5
- read_hidden: float32 [128, 16], replicated, may hold values from -0.5 to 0.5
- read_out: float32 [16], replicated, may hold values from -2 to 2
Outputs:
- site_energy: float32 [16384], P(('gx', 'gy', 'gz'))
- forces: float32 [3, 16384], P(None, ('gx', 'gy', 'gz'))
The draws below stay inside these ranges and needn't reach their ends.
Inputs may be any that keep to these rules, and one draw needn't show every extreme that they name: `send_list`: each domain's 8 * 4 entries name different owned atoms. `neighbours`: A slot names an owned atom other than the atom itself (rows below 128) or a row of one of the 56 cells with some q equal to 0 or 3. Atoms whose index within their domain is below 64 name owned atoms only. `edge_vectors`: live slots are 0.75 to 4.95 long, the others 5.25 to 5.95.
All inputs are finite; a program needn't handle non-finite values.
Results may differ from the reference program's by a relative error of at most 0.0041.
Values may be sent and summed in bfloat16 or wider, within the bound.
A program may use at most 128 MiB of HBM per device.

```python
import jax
import jax.numpy as jnp
from jax import lax

C = 128
RB = 8
RH = 64
RD = 16
SPECIES = 8
LAYERS = 2
M = 16
ATOM_DEV = 128
SEND = 4
ATOMS = 16384
N_GX = 4
N_GY = 8
N_GZ = 4


def draw_send_list(key, part):
    key = jax.random.fold_in(key, 11)
    domains = N_GX * N_GY * N_GZ
    domain_keys = jax.random.split(key, domains)
    orders = jax.vmap(lambda one_key: jax.random.permutation(one_key, ATOM_DEV))(domain_keys)
    chosen = orders[:, :8 * SEND]
    boxes = chosen.reshape(N_GX, N_GY, N_GZ, 2, 2, 2, SEND).transpose(0, 3, 1, 4, 2, 5, 6)
    return boxes.reshape(2 * N_GX, 2 * N_GY, 2 * N_GZ, SEND).astype(jnp.int32)


def draw_neighbours(key, part):
    key = jax.random.fold_in(key, 23)
    key_owned, key_cells, key_fix, key_row, key_pick = jax.random.split(key, 5)
    local_index = jnp.arange(ATOMS) % ATOM_DEV
    stepping = jax.random.randint(key_owned, (M, ATOMS), 1, ATOM_DEV)
    owned_row = (local_index[None, :] + stepping) % ATOM_DEV
    cell_index = jax.random.randint(key_cells, (3, M, ATOMS), 0, 4)
    middle = (cell_index >= 1) & (cell_index <= 2)
    interior = middle[0] & middle[1] & middle[2]
    cell_x = jnp.where(interior, 3 * jax.random.randint(key_fix, (M, ATOMS), 0, 2), cell_index[0])
    ghost_row = ATOM_DEV + ((cell_x * 4 + cell_index[1]) * 4 + cell_index[2]) * SEND + jax.random.randint(key_row, (M, ATOMS), 0, SEND)
    pick_ghost = (jax.random.randint(key_pick, (M, ATOMS), 0, 2) == 1) & (local_index[None, :] >= ATOM_DEV // 2)
    return jnp.where(pick_ghost, ghost_row, owned_row).astype(jnp.int32)


def draw_edge_vectors(key, part):
    key = jax.random.fold_in(key, 37)
    key_height, key_angle, key_count, key_length = jax.random.split(key, 4)
    height = jax.random.uniform(key_height, (M, ATOMS), jnp.float32, -1.0, 1.0)
    angle = jax.random.uniform(key_angle, (M, ATOMS), jnp.float32, -jnp.pi, jnp.pi)
    across = jnp.sqrt(jnp.maximum(1.0 - height * height, 0.0))
    direction = jnp.stack([across * jnp.cos(angle), across * jnp.sin(angle), height])
    live_count = jax.random.randint(key_count, (ATOMS,), M // 2, M + 1)
    live = jnp.arange(M)[:, None] < live_count[None, :]
    spread = jax.random.uniform(key_length, (M, ATOMS), jnp.float32, 0.0, 1.0)
    near = 0.75 + 4.2 * spread
    far = 5.25 + 0.7 * spread
    distance = jnp.where(live, near, far)
    return (direction * distance[None]).astype(jnp.float32)


def with_ends(array, stream_key, smallest, largest):
    longest = array.shape.index(max(array.shape))
    spots = []
    for shift in (0, 1):
        where = [jax.random.randint(jax.random.fold_in(stream_key, axis), (), 0, length) for axis, length in enumerate(array.shape)]
        where[longest] = (where[longest] + shift) % array.shape[longest]
        spots.append(tuple(where))
    return array.at[spots[0]].set(smallest).at[spots[1]].set(largest)


def centred(own_key, shape, scale, bound, dtype=jnp.bfloat16):
    values = jax.random.normal(own_key, shape, jnp.float32) * scale
    return jnp.minimum(jnp.maximum(values, -bound), bound).astype(dtype)


def setup_inputs(seed: int = 0) -> dict:
    splits = jax.random.split(jax.random.key(seed), 13)
    species = with_ends(jax.random.randint(splits[0], (ATOMS,), 0, SPECIES), jax.random.fold_in(splits[0], 1), 0, SPECIES - 1).astype(jnp.int32)
    send_list = draw_send_list(jax.random.fold_in(splits[12], 71), 0)
    neighbours = draw_neighbours(jax.random.fold_in(splits[12], 71), 0)
    edge_vectors = draw_edge_vectors(jax.random.fold_in(splits[12], 71), 0)
    embedding = centred(splits[4], (SPECIES, C), 1.0, 6.0)
    radial_in = centred(splits[5], (LAYERS, RB, RH), 4 ** -0.5, 3.0, jnp.float32)
    radial_mid = centred(splits[6], (LAYERS, RH, RH), (RH // 2) ** -0.5, 1.0, jnp.float32)
    radial_out = centred(splits[7], (LAYERS, RH, 3 * C), (RH // 4) ** -0.5, 1.5, jnp.float32)
    mixing = centred(splits[8], (LAYERS, 3 * C, C), (3 * C) ** -0.5, 0.3125, jnp.float32)
    read_linear = centred(splits[9], (C,), C ** -0.5, 0.5, jnp.float32)
    read_hidden = centred(splits[10], (C, RD), C ** -0.5, 0.5, jnp.float32)
    read_out = centred(splits[11], (RD,), (RD // 2) ** -0.5, 2.0, jnp.float32)
    return dict(species=species, send_list=send_list, neighbours=neighbours, edge_vectors=edge_vectors, embedding=embedding, radial_in=radial_in, radial_mid=radial_mid, radial_out=radial_out, mixing=mixing, read_linear=read_linear, read_hidden=read_hidden, read_out=read_out)


CUTOFF = 5.0
HIGHEST = lax.Precision.HIGHEST

def harmonics(unit):
    unit_x, unit_y, unit_z = (unit[0], unit[1], unit[2])
    root_three = 3.0 ** 0.5
    root_fifteen = 15.0 ** 0.5
    root_five = 5.0 ** 0.5
    degree_one = jnp.stack([root_three * unit_x, root_three * unit_y, root_three * unit_z])
    degree_two = jnp.stack([root_fifteen * unit_x * unit_y, root_fifteen * unit_y * unit_z, 0.5 * root_five * (3.0 * unit_z * unit_z - 1.0), root_fifteen * unit_x * unit_z, 0.5 * root_fifteen * (unit_x * unit_x - unit_y * unit_y)])
    return (degree_one, degree_two)

def interaction(extended, owned, vectors, links, weights):
    weight_in, weight_mid, weight_out, weight_mix = weights
    channels = owned.shape[1]
    length = jnp.sqrt(vectors[0] * vectors[0] + vectors[1] * vectors[1] + vectors[2] * vectors[2])
    unit = vectors / length
    ratio = length / CUTOFF
    envelope = jnp.where(ratio < 1.0, 1.0 - 21.0 * ratio ** 5 + 35.0 * ratio ** 6 - 15.0 * ratio ** 7, 0.0)
    orders = jnp.arange(1, weight_in.shape[0] + 1).astype(jnp.float32)
    basis = (2.0 / CUTOFF) ** 0.5 * jnp.sin(jnp.pi * ratio[..., None] * orders) / length[..., None]
    hidden_one = jax.nn.silu(jnp.matmul(basis, weight_in, precision=HIGHEST))
    hidden_two = jax.nn.silu(jnp.matmul(hidden_one, weight_mid, precision=HIGHEST))
    radial = jnp.matmul(hidden_two, weight_out, precision=HIGHEST) * envelope[..., None]
    gathered = extended[links]
    scale = 1.0 / links.shape[0] ** 0.5
    degree_one, degree_two = harmonics(unit)
    plain_sum = lax.optimization_barrier(jnp.sum(radial[..., :channels] * gathered, axis=0)) * scale
    vector_sum = jnp.einsum('msn,snc->mnc', degree_one, radial[..., channels:2 * channels] * gathered, precision=HIGHEST) * scale
    tensor_sum = jnp.einsum('msn,snc->mnc', degree_two, radial[..., 2 * channels:] * gathered, precision=HIGHEST) * scale
    invariants = jnp.concatenate([plain_sum, lax.optimization_barrier(jnp.sum(vector_sum * vector_sum, axis=0)), lax.optimization_barrier(jnp.sum(tensor_sum * tensor_sum, axis=0))], axis=1)
    return owned + jnp.dot(invariants, weight_mix, precision=HIGHEST)

def energies(extended, owned, vectors, links, weights, readout):
    read_linear, read_hidden, read_out = readout
    updated = interaction(extended, owned, vectors, links, weights)
    hidden = jax.nn.silu(jnp.dot(updated, read_hidden, precision=HIGHEST))
    return jnp.dot(owned, read_linear, precision=HIGHEST) + jnp.dot(hidden, read_out, precision=HIGHEST)

def fill_box(boxes):
    for offset in range(3):
        cell_axis = offset + 3
        extent = boxes.shape[cell_axis]
        lower_side = jnp.roll(boxes, 1, axis=offset)
        upper_side = jnp.roll(boxes, -1, axis=offset)
        boxes = jnp.concatenate([lax.slice_in_dim(lower_side, extent - 1, extent, axis=cell_axis), boxes, lax.slice_in_dim(upper_side, 0, 1, axis=cell_axis)], axis=cell_axis)
    return boxes

def fold_cells(padded, leading):
    for offset in range(3):
        cell_axis = leading + offset
        lower_half = jnp.take(padded, 2, axis=cell_axis) + jnp.take(padded, 0, axis=cell_axis)
        upper_half = jnp.take(padded, 3, axis=cell_axis) + jnp.take(padded, 5, axis=cell_axis)
        padded = jnp.stack([lower_half, upper_half], axis=cell_axis)
    return padded

def reference(species, send_list, neighbours, edge_vectors, embedding, radial_in, radial_mid, radial_out, mixing, read_linear, read_hidden, read_out):
    domains = N_GX * N_GY * N_GZ
    kinds_all = species.reshape(domains, ATOM_DEV)
    lists = send_list.reshape(N_GX, 2, N_GY, 2, N_GZ, 2, SEND).transpose(0, 2, 4, 1, 3, 5, 6).reshape(domains, 8 * SEND)
    link_all = neighbours.reshape(M, domains, ATOM_DEV).transpose(1, 0, 2)
    vector_all = edge_vectors.reshape(3, M, domains, ATOM_DEV).transpose(2, 0, 1, 3)
    table = (kinds_all.reshape(-1)[:, None] == jnp.arange(SPECIES)[None, :]).astype(jnp.bfloat16)
    start = jnp.dot(table, embedding, preferred_element_type=jnp.float32).astype(jnp.bfloat16).reshape(domains, ATOM_DEV, C)
    first_weights = (radial_in[0], radial_mid[0], radial_out[0], mixing[0])
    second_weights = (radial_in[1], radial_mid[1], radial_out[1], mixing[1])
    readout = (read_linear, read_hidden, read_out)

    def extend(values):
        boxes = jax.vmap(lambda rows, picks: rows[picks])(values, lists)
        boxes = boxes.reshape(N_GX, N_GY, N_GZ, 2, 2, 2, SEND, C)
        ghosts = fill_box(boxes).reshape(domains, 64 * SEND, C)
        return jnp.concatenate([values, ghosts], axis=1)
    ext_start = extend(start)

    def forward_first(item):
        extended, vectors, links = item
        return interaction(extended.astype(jnp.float32), extended[:ATOM_DEV].astype(jnp.float32), vectors, links, first_weights)
    first = lax.map(forward_first, (ext_start, vector_all, link_all)).astype(jnp.bfloat16)
    ext_first = extend(first)

    def backward_second(item):
        extended, vectors, links = item

        def energy_fn(ext_in, own_in, vec_in):
            return energies(ext_in, own_in, vec_in, links, second_weights, readout)
        values, pull = jax.vjp(energy_fn, extended.astype(jnp.float32), extended[:ATOM_DEV].astype(jnp.float32), vectors)
        cot_ext, cot_own, grad_vec = pull(jnp.ones_like(values))
        return (values, cot_ext, cot_own, grad_vec)
    site_energy, cot_ext, cot_own, grad_second = lax.map(backward_second, (ext_first, vector_all, link_all))
    ghost_cot = cot_ext[:, ATOM_DEV:].reshape(N_GX, N_GY, N_GZ, 4, 4, 4, SEND, C)
    back_cot = fold_cells(fill_box(ghost_cot), 3).reshape(domains, 8 * SEND, C)
    cot_first = cot_ext[:, :ATOM_DEV] + cot_own
    cot_first = jax.vmap(lambda total, picks, rows: total.at[picks].add(rows))(cot_first, lists, back_cot)

    def backward_first(item):
        extended, vectors, links, cotangent, grad_two = item

        def layer_fn(vec_in):
            return interaction(extended.astype(jnp.float32), extended[:ATOM_DEV].astype(jnp.float32), vec_in, links, first_weights)
        unused, pull = jax.vjp(layer_fn, vectors)
        gradient = pull(cotangent)[0] + grad_two
        partial_value = jnp.zeros((ATOM_DEV + 64 * SEND, 3), jnp.float32)
        partial_value = partial_value.at[:ATOM_DEV].add(lax.optimization_barrier(jnp.sum(gradient, axis=1)).T)
        partial_value = partial_value.at[links.reshape(-1)].add(-gradient.reshape(3, -1).T)
        return partial_value
    partials = lax.map(backward_first, (ext_start, vector_all, link_all, cot_first, grad_second))
    ghost_force = partials[:, ATOM_DEV:].reshape(N_GX, N_GY, N_GZ, 4, 4, 4, SEND, 3)
    back_force = fold_cells(fill_box(ghost_force), 3).reshape(domains, 8 * SEND, 3)
    forces = jax.vmap(lambda total, picks, rows: total.at[picks].add(rows))(partials[:, :ATOM_DEV], lists, back_force)
    return (site_energy.reshape(ATOMS), forces.transpose(2, 0, 1).reshape(3, ATOMS))
```

```python
import functools
import itertools

import jax
import jax.numpy as jnp
from jax import lax
from jax.experimental import pallas as pl
from jax.experimental.pallas import tpu as pltpu
from jax.sharding import PartitionSpec as P

CUTOFF = 5.0
AXES = ("gx", "gy", "gz")
F32 = jnp.float32
BF16 = jnp.bfloat16
MESH = pl.DeviceIdType.MESH
ROOT3 = 3.0**0.5
ROOT5 = 5.0**0.5
ROOT15 = 15.0**0.5
PI = 3.141592653589793


def plan_slabs(cell_rows):
    picks = {1: (1,), -1: (0,), 0: (0, 1)}
    slabs, offset = [], 0
    for count in (1, 2, 3):
        for step in itertools.product((-1, 0, 1), repeat=3):
            if sum(s != 0 for s in step) != count:
                continue
            cells = list(itertools.product(*[picks[s] for s in step]))
            if len(cells) == 1:
                cells.append(None)
            blocks = [tuple(cells[i : i + 2]) for i in range(0, len(cells), 2)]
            slabs.append((step, offset, 8 * len(blocks), blocks))
            offset += 8 * len(blocks)
    return slabs, offset


def ghost_row(step, cell, atoms, cell_rows):
    spots = [{1: 0, -1: 3, 0: c + 1}[s] for s, c in zip(step, cell)]
    return atoms + (16 * spots[0] + 4 * spots[1] + spots[2]) * cell_rows


def split_rows(x):
    high = x.astype(BF16).astype(F32)
    return jnp.concatenate([high, x - high, high], axis=0).astype(BF16)


def weight_rows(w):
    high = w.astype(BF16).astype(F32)
    return jnp.concatenate([high, high, w - high], axis=0)


def dot(a, b):
    return lax.dot_general(a, b, (((1,), (0,)), ((), ())), preferred_element_type=F32)


def dot_nt(a, b):
    return lax.dot_general(a, b, (((1,), (1,)), ((), ())), preferred_element_type=F32)


def loop(count, body):
    def step(i, carry):
        body(i)
        return carry

    lax.fori_loop(0, count, step, 0)


def kernel(
    sizes,
    species,
    send_list,
    neighbours,
    vectors,
    embedding,
    radial_in,
    radial_mid,
    radial_out,
    mixing,
    read_linear,
    read_hidden,
    read_out,
    site_out,
    force_out,
    basis,
    cut,
    harm,
    rad,
    drad,
    oh_own,
    oh_ghost,
    feat,
    amp,
    inv,
    cot_feat,
    acc_ref,
    grad_cat,
    sel,
    w_in,
    w_mid,
    w_out,
    mix_t,
    mix_c,
    first_ref,
    send_buf,
    recv_buf,
    send_sem,
    recv_sem,
):
    atoms = species.shape[1]
    half = atoms // 2
    channels = embedding.shape[1]
    pairs = neighbours.shape[0] // 2
    cell_rows = send_list.shape[3]
    hidden = radial_mid.shape[1]
    slabs, ghosts = plan_slabs(cell_rows)
    me = [lax.axis_index(axis) for axis in AXES]

    def at(step):
        return tuple(
            m if s == 0 else lax.rem(m + (s + n), n) for m, s, n in zip(me, step, sizes)
        )

    barrier = pltpu.get_barrier_semaphore()
    for step, _, _, _ in slabs:
        pl.semaphore_signal(barrier, inc=1, device_id=at(step), device_id_type=MESH)

    def send(phase, back):
        for step, offset, rows, _ in slabs:
            goal = tuple(-s for s in step) if back else step
            pltpu.make_async_remote_copy(
                src_ref=send_buf.at[phase, pl.ds(offset, rows)],
                dst_ref=recv_buf.at[phase, pl.ds(offset, rows)],
                send_sem=send_sem.at[phase],
                recv_sem=recv_sem.at[phase],
                device_id=at(goal),
                device_id_type=MESH,
            ).start()

    def wait_in(phase):
        whole = recv_buf.at[phase]
        pltpu.make_async_copy(whole, whole, recv_sem.at[phase]).wait()

    def wait_out(phase):
        whole = send_buf.at[phase]
        pltpu.make_async_copy(whole, whole, send_sem.at[phase]).wait()

    lane = lax.broadcasted_iota(jnp.int32, (8, atoms), 1)
    sub = lax.broadcasted_iota(jnp.int32, (8, atoms), 0)
    low8 = lane < half

    def low_of(x):
        return lax.broadcasted_iota(jnp.int32, x.shape, 1) < half

    def turn(x):
        return pltpu.roll(x, half, 1)

    def dup(x, group):
        if group == 0:
            return jnp.where(low_of(x), x, turn(x))
        return jnp.where(low_of(x), turn(x), x)

    def paired(x):
        top, bottom = x[:pairs], x[pairs:]
        return (
            jnp.where(low8, top, turn(bottom)),
            jnp.where(low8, turn(top), bottom),
        )

    cell_ids = {}
    spot = sub % cell_rows
    for cell in itertools.product((0, 1), repeat=3):
        value = jnp.full((8, atoms), send_list[cell + (0,)], jnp.int32)
        for k in range(1, cell_rows):
            value = jnp.where(spot == k, send_list[cell + (k,)], value)
        cell_ids[cell] = value
    cell_ids[None] = jnp.full((8, atoms), -1, jnp.int32)
    row_ids = []
    chosen = []
    for step, offset, rows, blocks in slabs:
        for cell_a, cell_b in blocks:
            ids = jnp.where(sub < cell_rows, cell_ids[cell_a], cell_ids[cell_b])
            chosen.append(jnp.where(ids == lane, 1.0, 0.0))
            base_a = ghost_row(step, cell_a, atoms, cell_rows) + sub
            if cell_b is None:
                base_b = jnp.full((8, atoms), -1, jnp.int32)
            else:
                base_b = ghost_row(step, cell_b, atoms, cell_rows) + sub - cell_rows
            row_ids.append(jnp.where(sub < cell_rows, base_a, base_b))
    sel[...] = jnp.concatenate(chosen, axis=0).astype(BF16)

    kinds = jnp.where(sub == jnp.broadcast_to(species[...], (8, atoms)), 1.0, 0.0).astype(BF16)
    emb_t = embedding[...].astype(F32).T.astype(BF16)
    start_t = dot(emb_t, kinds)
    send_buf[0] = dot_nt(sel[...], start_t.astype(BF16))

    for t in range(2):
        pad = jnp.zeros((8, hidden), F32)
        w_in[t * hidden : (t + 1) * hidden] = (
            jnp.concatenate([weight_rows(radial_in[t]), pad], axis=0).T.astype(BF16)
        )
        w_mid[t] = weight_rows(radial_mid[t]).T.astype(BF16)
        w_out[t] = weight_rows(radial_out[t]).T.astype(BF16)

    vec = [paired(vectors[k]) for k in range(3)]
    nbr = paired(neighbours[...])
    geo = []
    for g in range(2):
        x, y, z = vec[0][g], vec[1][g], vec[2][g]
        length = jnp.sqrt(x * x + y * y + z * z)
        over = 1.0 / length
        nx, ny, nz = x * over, y * over, z * over
        geo.append((nx, ny, nz, over))
        u = length * (1.0 / CUTOFF)
        u2 = u * u
        u4 = u2 * u2
        u5 = u4 * u
        inside = u < 1.0
        env = 1.0 - 21.0 * u5 + 35.0 * u5 * u - 15.0 * u5 * u2
        denv = (-105.0 / CUTOFF) * u4 * (1.0 - u) * (1.0 - u)
        cut[g, 0] = jnp.where(inside, 0.25 * env, 0.0)
        cut[g, 1] = jnp.where(inside, 0.25 * denv, 0.0)
        theta = PI * u
        sin1, cos1 = jnp.sin(theta), jnp.cos(theta)
        twice = 2.0 * cos1
        s_old, s_now = jnp.zeros_like(sin1), sin1
        c_old, c_now = jnp.ones_like(cos1), cos1
        amp0 = (2.0 / CUTOFF) ** 0.5
        for k in range(1, 9):
            base = amp0 * s_now * over
            slope = (amp0 * k * PI / CUTOFF * c_now - base) * over
            basis[g, 0, (k - 1) * 8 : k * 8] = base
            basis[g, 1, (k - 1) * 8 : k * 8] = slope
            s_old, s_now = s_now, twice * s_now - s_old
            c_old, c_now = c_now, twice * c_now - c_old
        ylm = (
            ROOT3 * nx,
            ROOT3 * ny,
            ROOT3 * nz,
            ROOT15 * nx * ny,
            ROOT15 * ny * nz,
            0.5 * ROOT5 * (3.0 * nz * nz - 1.0),
            ROOT15 * nx * nz,
            0.5 * ROOT15 * (nx * nx - ny * ny),
        )
        for m in range(8):
            for p in range(pairs):
                harm[g * pairs + p, m * 8 : (m + 1) * 8] = jnp.broadcast_to(
                    ylm[m][p : p + 1], (8, atoms)
                )

    own_rows = jnp.concatenate([sub + 8 * b for b in range(atoms // 8)], axis=0)
    all_rows = jnp.concatenate([own_rows] + row_ids, axis=0)
    for p in range(pairs):
        lanes = slice(p * atoms, (p + 1) * atoms)
        oh_own[:, lanes] = jnp.where(own_rows == nbr[0][p : p + 1], 1.0, 0.0).astype(BF16)
        oh_ghost[:, lanes] = jnp.where(all_rows == nbr[1][p : p + 1], 1.0, 0.0).astype(BF16)

    pl.semaphore_wait(barrier, len(slabs))
    send(0, False)

    def silu_pair(x, dx):
        gate = 0.5 + 0.5 * jnp.tanh(0.5 * x)
        value = x * gate
        return value, gate * (1.0 + x - value) * dx

    def radial(g):
        def chunk(j):
            def wide(ref, kind):
                return jnp.concatenate(
                    [ref[g, kind, pl.ds(2 * j + i, 8, stride=8), :] for i in range(2)], axis=1
                )

            def row(kind):
                return jnp.concatenate(
                    [cut[g, kind, pl.ds(2 * j + i, 1), :] for i in range(2)], axis=1
                )

            env, denv = row(0), row(1)
            pad = jnp.zeros((8, 2 * atoms), BF16)

            def first_dot(x):
                high = x.astype(BF16).astype(F32)
                full = jnp.concatenate([high, x - high, high, jnp.zeros_like(x)], axis=0)
                return dot(w_in[...], full.astype(BF16))

            one, done = silu_pair(first_dot(wide(basis, 0)), first_dot(wide(basis, 1)))
            for t in range(2):
                rows = slice(t * hidden, (t + 1) * hidden)
                two, dtwo = silu_pair(
                    dot(w_mid[t], split_rows(one[rows])), dot(w_mid[t], split_rows(done[rows]))
                )
                value = dot(w_out[t], split_rows(env * two))
                slope = dot(w_out[t], split_rows(denv * two + env * dtwo))
                for i in range(2):
                    lanes = slice(i * atoms, (i + 1) * atoms)
                    rad[(t * 2 + g) * pairs + 2 * j + i] = value[:, lanes]
                    drad[(t * 2 + g) * pairs + 2 * j + i] = slope[:, lanes]

        loop(pairs // 2, chunk)

    radial(0)
    radial(1)
    for t in range(2):
        mix_t[t] = weight_rows(mixing[t]).T.astype(BF16)
        high = mixing[t].astype(BF16).astype(F32)
        mix_c[t] = jnp.concatenate([high, high, mixing[t] - high], axis=1).astype(BF16)
    rl_col = jnp.broadcast_to(read_linear[...], (channels, channels)).T
    rh = read_hidden[...]
    rh_t = weight_rows(rh).T.astype(BF16)
    rh_high = rh.astype(BF16).astype(F32)
    rh_c = jnp.concatenate([rh_high, rh_high, rh - rh_high], axis=1).astype(BF16)
    ro_col = jnp.broadcast_to(read_out[...], (channels, read_out.shape[1])).T

    def gather(t, g, own_t, ghost_t):
        base = (t * 2 + g) * pairs

        def chunk(j):
            lanes = pl.ds(pl.multiple_of(j * 2 * atoms, 2 * atoms), 2 * atoms)
            if g == 0:
                out = dot(own_t, oh_own[:, lanes])
            else:
                out = dot(own_t, oh_ghost[:atoms, lanes]) + dot(ghost_t, oh_ghost[atoms:, lanes])
            feat[base + 2 * j] = out[:, :atoms]
            feat[base + 2 * j + 1] = out[:, atoms:]

        loop(pairs // 2, chunk)

    def twin(y):
        return jnp.concatenate([y, y], axis=0)

    def forward(t, g):
        which = t * 2 + g
        base = which * pairs

        def block(b):
            row = pl.multiple_of(b * 16, 16)

            def rows(l):
                return pl.ds(pl.multiple_of(row + l * channels, 16), 16)

            total = [jnp.zeros((16, atoms), F32) for _ in range(9)]
            for p in range(pairs):
                v = feat[base + p, rows(0)]
                parts = [rad[base + p, rows(l)] * v for l in range(3)]
                total[0] = total[0] + parts[0]
                for m in range(8):
                    y = twin(harm[g * pairs + p, m * 8 : (m + 1) * 8])
                    total[1 + m] = total[1 + m] + y * parts[1 if m < 3 else 2]
            total = [a + turn(a) for a in total]
            for m in range(1, 9):
                amp[which, m, rows(0)] = total[m]
            inv[rows(0)] = total[0]
            inv[rows(1)] = sum(a * a for a in total[1:4])
            inv[rows(2)] = sum(a * a for a in total[4:9])

        loop(channels // 16, block)

    def back_amp(t, g, dinv):
        which = t * 2 + g
        inv[...] = dinv

        def block(b):
            row = pl.multiple_of(b * 16, 16)

            def rows(l):
                return pl.ds(pl.multiple_of(row + l * channels, 16), 16)

            amp[which, 0, rows(0)] = inv[rows(0)]
            d1 = 2.0 * inv[rows(1)]
            d2 = 2.0 * inv[rows(2)]
            for m in range(1, 9):
                amp[which, m, rows(0)] = amp[which, m, rows(0)] * (d1 if m < 4 else d2)

        loop(channels // 16, block)

    def backward(t, g):
        which = t * 2 + g
        base = which * pairs

        def slot(p):
            ys = [twin(harm[g * pairs + p, m * 8 : (m + 1) * 8]) for m in range(8)]
            total = [jnp.zeros((16, atoms), F32) for _ in range(9)]
            lanes = pl.ds(pl.multiple_of(p * atoms, atoms), atoms)
            for c in range(0, channels, 16):
                rows = slice(c, c + 16)
                v = feat[base + p, rows]
                r = [rad[base + p, l * channels + c : l * channels + c + 16] for l in range(3)]
                q = [drad[base + p, l * channels + c : l * channels + c + 16] for l in range(3)]
                d = [amp[which, m, rows] for m in range(9)]
                t1 = ys[0] * d[1] + ys[1] * d[2] + ys[2] * d[3]
                t2 = ys[3] * d[4] + ys[4] * d[5] + ys[5] * d[6] + ys[6] * d[7] + ys[7] * d[8]
                if t == 1:
                    cot_feat[g, rows, lanes] = (r[0] * d[0] + r[1] * t1 + r[2] * t2).astype(BF16)
                total[0] = total[0] + v * (q[0] * d[0] + q[1] * t1 + q[2] * t2)
                p1, p2 = v * r[1], v * r[2]
                for m in range(1, 9):
                    total[m] = total[m] + (p1 if m < 4 else p2) * d[m]
            for m in range(9):
                part = total[m][:8] + total[m][8:]
                spots = pl.ds(pl.multiple_of(p * 8, 8), 8)
                if t == 1:
                    acc_ref[g, m, spots] = part
                else:
                    acc_ref[g, m, spots] = acc_ref[g, m, spots] + part

        loop(pairs, slot)

    start_b = start_t.astype(BF16)
    gather(0, 0, start_b, None)
    forward(0, 0)
    inv_own = inv[...]
    wait_in(0)
    gather(0, 1, start_b, recv_buf[0].T.astype(BF16))
    forward(0, 1)
    inv_both = jnp.where(low_of(inv_own), inv_own, inv[...])
    first_b = (start_t + dot(mix_t[0], split_rows(inv_both))).astype(BF16)
    send_buf[1] = dot_nt(sel[...], first_b)
    send(1, False)
    first_ref[...] = first_b.astype(F32)

    def energy(g):
        own = dup(first_ref[...], g)
        second = own + dot(mix_t[1], split_rows(inv[...]))
        act = dot(rh_t, split_rows(second))
        gate = 0.5 + 0.5 * jnp.tanh(0.5 * act)
        value = act * gate
        site = jnp.sum(rl_col * own, axis=0, keepdims=True) + jnp.sum(
            ro_col * value, axis=0, keepdims=True
        )
        dact = ro_col * gate * (1.0 + act - value)
        dsecond = dot(rh_c, split_rows(dact))
        return site, rl_col + dsecond, dot(mix_c[1], split_rows(dsecond))

    gather(1, 0, first_b, None)
    forward(1, 0)
    site_own, cot_own, dinv = energy(0)
    back_amp(1, 0, dinv)
    backward(1, 0)
    wait_in(1)
    gather(1, 1, first_ref[...].astype(BF16), recv_buf[1].T.astype(BF16))
    forward(1, 1)
    site_ghost, cot_ghost, dinv = energy(1)
    back_amp(1, 1, dinv)
    backward(1, 1)
    send_buf[2] = dot_nt(oh_ghost[atoms:], cot_feat[1])
    send(2, True)
    site_out[...] = jnp.where(low_of(site_own), site_own, site_ghost)
    cot = jnp.where(low_of(cot_own), cot_own, cot_ghost)
    cot = cot + dot_nt(cot_feat[0], oh_own[...]) + dot_nt(cot_feat[1], oh_ghost[:atoms])
    send_buf[3] = jnp.zeros((ghosts, atoms), F32)
    wait_in(2)
    back = recv_buf[2].T
    high = back.astype(BF16).astype(F32)
    parts = dot(jnp.concatenate([high, back - high], axis=0).astype(BF16), sel[...])
    cot = cot + parts[:channels] + parts[channels:]

    for g in range(2):
        back_amp(0, g, dot(mix_c[0], split_rows(dup(cot, g))))
        backward(0, g)

    sums = []
    for g in range(2):
        d = []
        for m in range(9):
            d.append(sum(acc_ref[g, m, pl.ds(j, pairs, stride=8), :] for j in range(8)))
        nx, ny, nz, over = geo[g]
        gx = ROOT3 * d[1] + ROOT15 * (ny * d[4] + nz * d[7] + nx * d[8])
        gy = ROOT3 * d[2] + ROOT15 * (nx * d[4] + nz * d[5] - ny * d[8])
        gz = ROOT3 * d[3] + ROOT15 * (ny * d[5] + nx * d[7]) + (3.0 * ROOT5) * nz * d[6]
        along = d[0] - (nx * gx + ny * gy + nz * gz) * over
        grad = [n * along + c * over for n, c in ((nx, gx), (ny, gy), (nz, gz))]
        folded = []
        for k in range(3):
            one = jnp.sum(grad[k], axis=0, keepdims=True)
            folded.append(one + turn(one))
            basis[g, 0, k * 8 : (k + 1) * 8] = -grad[k]
        sums.append(folded)
        basis[g, 0, 24:64] = jnp.zeros((40, atoms), F32)
        for p in range(pairs):
            row = basis[g, 0, pl.ds(p, 8, stride=8), :]
            high = row.astype(BF16).astype(F32)
            grad_cat[g, :, p * atoms : (p + 1) * atoms] = jnp.concatenate(
                [high, row - high], axis=0
            ).astype(BF16)
    send_buf[3, :, 0:16] = dot_nt(oh_ghost[atoms:], grad_cat[1])
    send(3, True)
    local = dot_nt(grad_cat[0], oh_own[...]) + dot_nt(grad_cat[1], oh_ghost[:atoms])
    local = local[:8] + local[8:]
    mine = jnp.concatenate(
        [jnp.where(low_of(sums[0][k]), sums[0][k], sums[1][k]) for k in range(3)], axis=0
    )
    local = local[:3] + mine
    wait_in(3)
    back = recv_buf[3].T
    back = back[:8] + back[8:16]
    high = back.astype(BF16).astype(F32)
    mid = (back - high).astype(BF16).astype(F32)
    parts = dot(jnp.concatenate([high, mid, back - high - mid], axis=0).astype(BF16), sel[...])
    force_out[...] = local + (parts[:8] + parts[8:16] + parts[16:24])[:3]
    for phase in range(4):
        wait_out(phase)


def solution(mesh):
    sizes = tuple(mesh.shape[axis] for axis in AXES)

    def body(
        species,
        send_list,
        neighbours,
        edge_vectors,
        embedding,
        radial_in,
        radial_mid,
        radial_out,
        mixing,
        read_linear,
        read_hidden,
        read_out,
    ):
        atoms = species.shape[0]
        channels = embedding.shape[1]
        slots = neighbours.shape[0]
        pairs = slots // 2
        hidden = radial_mid.shape[1]
        ghosts = plan_slabs(send_list.shape[3])[1]
        vmem = pl.BlockSpec(memory_space=pltpu.VMEM)
        smem = pl.BlockSpec(memory_space=pltpu.SMEM)
        site, forces = pl.pallas_call(
            functools.partial(kernel, sizes),
            out_shape=(
                jax.ShapeDtypeStruct((1, atoms), F32),
                jax.ShapeDtypeStruct((3, atoms), F32),
            ),
            in_specs=[vmem, smem] + [vmem] * 10,
            out_specs=(vmem, vmem),
            scratch_shapes=[
                pltpu.VMEM((2, 2, 8 * pairs, atoms), F32),
                pltpu.VMEM((2, 2, pairs, atoms), F32),
                pltpu.VMEM((2 * pairs, 64, atoms), F32),
                pltpu.VMEM((4 * pairs, 3 * channels, atoms), F32),
                pltpu.VMEM((4 * pairs, 3 * channels, atoms), F32),
                pltpu.VMEM((atoms, pairs * atoms), BF16),
                pltpu.VMEM((atoms + ghosts, pairs * atoms), BF16),
                pltpu.VMEM((4 * pairs, channels, atoms), F32),
                pltpu.VMEM((4, 9, channels, atoms), F32),
                pltpu.VMEM((3 * channels, atoms), F32),
                pltpu.VMEM((2, channels, pairs * atoms), BF16),
                pltpu.VMEM((2, 9, 8 * pairs, atoms), F32),
                pltpu.VMEM((2, 16, pairs * atoms), BF16),
                pltpu.VMEM((ghosts, atoms), BF16),
                pltpu.VMEM((2 * hidden, 32), BF16),
                pltpu.VMEM((2, hidden, 3 * hidden), BF16),
                pltpu.VMEM((2, 3 * channels, 3 * hidden), BF16),
                pltpu.VMEM((2, channels, 9 * channels), BF16),
                pltpu.VMEM((2, 3 * channels, 3 * channels), BF16),
                pltpu.VMEM((channels, atoms), F32),
                pltpu.VMEM((4, ghosts, channels), F32),
                pltpu.VMEM((4, ghosts, channels), F32),
                pltpu.SemaphoreType.DMA((4,)),
                pltpu.SemaphoreType.DMA((4,)),
            ],
            compiler_params=pltpu.CompilerParams(
                collective_id=0, has_side_effects=True, vmem_limit_bytes=56 * 1024 * 1024
            ),
        )(
            species.reshape(1, atoms),
            send_list,
            neighbours,
            edge_vectors,
            embedding,
            radial_in,
            radial_mid,
            radial_out,
            mixing,
            read_linear.reshape(1, channels),
            read_hidden,
            read_out.reshape(1, read_out.shape[0]),
        )
        return site.reshape(atoms), forces

    in_specs = (
        P(AXES),
        P("gx", "gy", "gz", None),
        P(None, AXES),
        P(None, None, AXES),
        P(),
        P(),
        P(),
        P(),
        P(),
        P(),
        P(),
        P(),
    )
    out_specs = (P(AXES), P(None, AXES))
    return jax.shard_map(body, mesh=mesh, in_specs=in_specs, out_specs=out_specs, check_vma=False)
```

```python
import functools
import itertools

import jax
import jax.numpy as jnp
from jax import lax
from jax.experimental import pallas as pl
from jax.experimental.pallas import tpu as pltpu
from jax.sharding import PartitionSpec as P

CUTOFF = 5.0
AXES = ("gx", "gy", "gz")
F32 = jnp.float32
BF16 = jnp.bfloat16
MESH = pl.DeviceIdType.MESH
ROOT3 = 3.0**0.5
ROOT5 = 5.0**0.5
ROOT15 = 15.0**0.5
PI = 3.141592653589793


def plan_slabs(cell_rows):
    picks = {1: (1,), -1: (0,), 0: (0, 1)}
    slabs, offset = [], 0
    for count in (1, 2, 3):
        for step in itertools.product((-1, 0, 1), repeat=3):
            if sum(s != 0 for s in step) != count:
                continue
            cells = list(itertools.product(*[picks[s] for s in step]))
            if len(cells) == 1:
                cells.append(None)
            blocks = [tuple(cells[i : i + 2]) for i in range(0, len(cells), 2)]
            slabs.append((step, offset, 8 * len(blocks), blocks))
            offset += 8 * len(blocks)
    return slabs, offset


def ghost_row(step, cell, atoms, cell_rows):
    spots = [{1: 0, -1: 3, 0: c + 1}[s] for s, c in zip(step, cell)]
    return atoms + (16 * spots[0] + 4 * spots[1] + spots[2]) * cell_rows


def split_rows(x):
    high = x.astype(BF16).astype(F32)
    return jnp.concatenate([high, x - high, high], axis=0).astype(BF16)


def weight_rows(w):
    high = w.astype(BF16).astype(F32)
    return jnp.concatenate([high, high, w - high], axis=0)


def dot(a, b):
    return lax.dot_general(a, b, (((1,), (0,)), ((), ())), preferred_element_type=F32)


def dot_nt(a, b):
    return lax.dot_general(a, b, (((1,), (1,)), ((), ())), preferred_element_type=F32)


def mult(x, n):
    return x if isinstance(x, int) else pl.multiple_of(x, n)


def loop(count, body):
    for i in range(count):
        body(i)


def kernel(
    sizes,
    species,
    send_list,
    neighbours,
    vectors,
    embedding,
    radial_in,
    radial_mid,
    radial_out,
    mixing,
    read_linear,
    read_hidden,
    read_out,
    site_out,
    force_out,
    basis,
    cut,
    harm,
    rad,
    drad,
    oh_own,
    oh_ghost,
    feat,
    amp,
    inv,
    cot_feat,
    acc_ref,
    grad_cat,
    sel,
    w_in,
    w_mid,
    w_out,
    mix_t,
    mix_c,
    first_ref,
    send_buf,
    recv_buf,
    send_sem,
    recv_sem,
):
    atoms = species.shape[1]
    half = atoms // 2
    channels = embedding.shape[1]
    pairs = neighbours.shape[0] // 2
    cell_rows = send_list.shape[3]
    hidden = radial_mid.shape[1]
    slabs, ghosts = plan_slabs(cell_rows)
    me = [lax.axis_index(axis) for axis in AXES]

    def at(step):
        return tuple(
            m if s == 0 else lax.rem(m + (s + n), n) for m, s, n in zip(me, step, sizes)
        )

    barrier = pltpu.get_barrier_semaphore()
    for step, _, _, _ in slabs:
        pl.semaphore_signal(barrier, inc=1, device_id=at(step), device_id_type=MESH)

    def send(phase, back):
        for step, offset, rows, _ in slabs:
            goal = tuple(-s for s in step) if back else step
            pltpu.make_async_remote_copy(
                src_ref=send_buf.at[phase, pl.ds(offset, rows)],
                dst_ref=recv_buf.at[phase, pl.ds(offset, rows)],
                send_sem=send_sem.at[phase],
                recv_sem=recv_sem.at[phase],
                device_id=at(goal),
                device_id_type=MESH,
            ).start()

    def wait_in(phase):
        whole = recv_buf.at[phase]
        pltpu.make_async_copy(whole, whole, recv_sem.at[phase]).wait()

    def wait_out(phase):
        whole = send_buf.at[phase]
        pltpu.make_async_copy(whole, whole, send_sem.at[phase]).wait()

    lane = lax.broadcasted_iota(jnp.int32, (8, atoms), 1)
    sub = lax.broadcasted_iota(jnp.int32, (8, atoms), 0)
    low8 = lane < half

    def low_of(x):
        return lax.broadcasted_iota(jnp.int32, x.shape, 1) < half

    def turn(x):
        return pltpu.roll(x, half, 1)

    def dup(x, group):
        if group == 0:
            return jnp.where(low_of(x), x, turn(x))
        return jnp.where(low_of(x), turn(x), x)

    def paired(x):
        top, bottom = x[:pairs], x[pairs:]
        return (
            jnp.where(low8, top, turn(bottom)),
            jnp.where(low8, turn(top), bottom),
        )

    cell_ids = {}
    spot = sub % cell_rows
    for cell in itertools.product((0, 1), repeat=3):
        value = jnp.full((8, atoms), send_list[cell + (0,)], jnp.int32)
        for k in range(1, cell_rows):
            value = jnp.where(spot == k, send_list[cell + (k,)], value)
        cell_ids[cell] = value
    cell_ids[None] = jnp.full((8, atoms), -1, jnp.int32)
    row_ids = []
    chosen = []
    for step, offset, rows, blocks in slabs:
        for cell_a, cell_b in blocks:
            ids = jnp.where(sub < cell_rows, cell_ids[cell_a], cell_ids[cell_b])
            chosen.append(jnp.where(ids == lane, 1.0, 0.0))
            base_a = ghost_row(step, cell_a, atoms, cell_rows) + sub
            if cell_b is None:
                base_b = jnp.full((8, atoms), -1, jnp.int32)
            else:
                base_b = ghost_row(step, cell_b, atoms, cell_rows) + sub - cell_rows
            row_ids.append(jnp.where(sub < cell_rows, base_a, base_b))
    sel[...] = jnp.concatenate(chosen, axis=0).astype(BF16)

    kinds = jnp.where(sub == jnp.broadcast_to(species[...], (8, atoms)), 1.0, 0.0).astype(BF16)
    emb_t = embedding[...].astype(F32).T.astype(BF16)
    start_t = dot(emb_t, kinds)
    send_buf[0] = dot_nt(sel[...], start_t.astype(BF16))

    for t in range(2):
        pad = jnp.zeros((8, hidden), F32)
        w_in[t * hidden : (t + 1) * hidden] = (
            jnp.concatenate([weight_rows(radial_in[t]), pad], axis=0).T.astype(BF16)
        )
        w_mid[t] = weight_rows(radial_mid[t]).T.astype(BF16)
        w_out[t] = weight_rows(radial_out[t]).T.astype(BF16)

    vec = [paired(vectors[k]) for k in range(3)]
    nbr = paired(neighbours[...])
    geo = []
    for g in range(2):
        x, y, z = vec[0][g], vec[1][g], vec[2][g]
        length = jnp.sqrt(x * x + y * y + z * z)
        over = 1.0 / length
        nx, ny, nz = x * over, y * over, z * over
        geo.append((nx, ny, nz, over))
        u = length * (1.0 / CUTOFF)
        u2 = u * u
        u4 = u2 * u2
        u5 = u4 * u
        inside = u < 1.0
        env = 1.0 - 21.0 * u5 + 35.0 * u5 * u - 15.0 * u5 * u2
        denv = (-105.0 / CUTOFF) * u4 * (1.0 - u) * (1.0 - u)
        cut[g, 0] = jnp.where(inside, 0.25 * env, 0.0)
        cut[g, 1] = jnp.where(inside, 0.25 * denv, 0.0)
        theta = PI * u
        sin1, cos1 = jnp.sin(theta), jnp.cos(theta)
        twice = 2.0 * cos1
        s_old, s_now = jnp.zeros_like(sin1), sin1
        c_old, c_now = jnp.ones_like(cos1), cos1
        amp0 = (2.0 / CUTOFF) ** 0.5
        for k in range(1, 9):
            base = amp0 * s_now * over
            slope = (amp0 * k * PI / CUTOFF * c_now - base) * over
            basis[g, 0, (k - 1) * 8 : k * 8] = base
            basis[g, 1, (k - 1) * 8 : k * 8] = slope
            s_old, s_now = s_now, twice * s_now - s_old
            c_old, c_now = c_now, twice * c_now - c_old
        ylm = (
            ROOT3 * nx,
            ROOT3 * ny,
            ROOT3 * nz,
            ROOT15 * nx * ny,
            ROOT15 * ny * nz,
            0.5 * ROOT5 * (3.0 * nz * nz - 1.0),
            ROOT15 * nx * nz,
            0.5 * ROOT15 * (nx * nx - ny * ny),
        )
        for m in range(8):
            for p in range(pairs):
                harm[g * pairs + p, m * 8 : (m + 1) * 8] = jnp.broadcast_to(
                    ylm[m][p : p + 1], (8, atoms)
                )

    own_rows = jnp.concatenate([sub + 8 * b for b in range(atoms // 8)], axis=0)
    all_rows = jnp.concatenate([own_rows] + row_ids, axis=0)
    for p in range(pairs):
        lanes = slice(p * atoms, (p + 1) * atoms)
        oh_own[:, lanes] = jnp.where(own_rows == nbr[0][p : p + 1], 1.0, 0.0).astype(BF16)
        oh_ghost[:, lanes] = jnp.where(all_rows == nbr[1][p : p + 1], 1.0, 0.0).astype(BF16)

    pl.semaphore_wait(barrier, len(slabs))
    send(0, False)

    def silu_pair(x, dx):
        gate = 0.5 + 0.5 * jnp.tanh(0.5 * x)
        value = x * gate
        return value, gate * (1.0 + x - value) * dx

    def radial(g):
        def chunk(j):
            def wide(ref, kind):
                return jnp.concatenate(
                    [ref[g, kind, pl.ds(2 * j + i, 8, stride=8), :] for i in range(2)], axis=1
                )

            def row(kind):
                return jnp.concatenate(
                    [cut[g, kind, pl.ds(2 * j + i, 1), :] for i in range(2)], axis=1
                )

            env, denv = row(0), row(1)
            pad = jnp.zeros((8, 2 * atoms), BF16)

            def first_dot(x):
                high = x.astype(BF16).astype(F32)
                full = jnp.concatenate([high, x - high, high, jnp.zeros_like(x)], axis=0)
                return dot(w_in[...], full.astype(BF16))

            one, done = silu_pair(first_dot(wide(basis, 0)), first_dot(wide(basis, 1)))
            for t in range(2):
                rows = slice(t * hidden, (t + 1) * hidden)
                two, dtwo = silu_pair(
                    dot(w_mid[t], split_rows(one[rows])), dot(w_mid[t], split_rows(done[rows]))
                )
                value = dot(w_out[t], split_rows(env * two))
                slope = dot(w_out[t], split_rows(denv * two + env * dtwo))
                for i in range(2):
                    lanes = slice(i * atoms, (i + 1) * atoms)
                    rad[(t * 2 + g) * pairs + 2 * j + i] = value[:, lanes]
                    drad[(t * 2 + g) * pairs + 2 * j + i] = slope[:, lanes]

        loop(pairs // 2, chunk)

    radial(0)
    radial(1)
    for t in range(2):
        mix_t[t] = weight_rows(mixing[t]).T.astype(BF16)
        high = mixing[t].astype(BF16).astype(F32)
        mix_c[t] = jnp.concatenate([high, high, mixing[t] - high], axis=1).astype(BF16)
    rl_col = jnp.broadcast_to(read_linear[...], (channels, channels)).T
    rh = read_hidden[...]
    rh_high = rh.astype(BF16).astype(F32)
    rh_t = jnp.concatenate([rh_high, rh_high, rh - rh_high], axis=1).astype(BF16)
    rh_c = weight_rows(rh).T.astype(BF16)
    ro_col = jnp.broadcast_to(read_out[...], (channels, read_out.shape[1])).T

    def gather(t, g, own_t, ghost_t):
        base = (t * 2 + g) * pairs

        def chunk(j):
            lanes = pl.ds(mult(j * 2 * atoms, 2 * atoms), 2 * atoms)
            if g == 0:
                out = dot(own_t, oh_own[:, lanes])
            else:
                out = dot(own_t, oh_ghost[:atoms, lanes]) + dot(ghost_t, oh_ghost[atoms:, lanes])
            feat[base + 2 * j] = out[:, :atoms]
            feat[base + 2 * j + 1] = out[:, atoms:]

        loop(pairs // 2, chunk)

    def twin(y):
        return jnp.concatenate([y, y], axis=0)

    def forward(t, g):
        which = t * 2 + g
        base = which * pairs

        def block(b):
            row = mult(b * 16, 16)

            def rows(l):
                return pl.ds(mult(row + l * channels, 16), 16)

            total = [jnp.zeros((16, atoms), F32) for _ in range(9)]
            for p in range(pairs):
                v = feat[base + p, rows(0)]
                parts = [rad[base + p, rows(l)] * v for l in range(3)]
                total[0] = total[0] + parts[0]
                for m in range(8):
                    y = twin(harm[g * pairs + p, m * 8 : (m + 1) * 8])
                    total[1 + m] = total[1 + m] + y * parts[1 if m < 3 else 2]
            total = [a + turn(a) for a in total]
            for m in range(1, 9):
                amp[which, m, rows(0)] = total[m]
            inv[rows(0)] = total[0]
            inv[rows(1)] = sum(a * a for a in total[1:4])
            inv[rows(2)] = sum(a * a for a in total[4:9])

        loop(channels // 16, block)

    def back_amp(t, g, dinv):
        which = t * 2 + g
        inv[...] = dinv

        def block(b):
            row = mult(b * 16, 16)

            def rows(l):
                return pl.ds(mult(row + l * channels, 16), 16)

            amp[which, 0, rows(0)] = inv[rows(0)]
            d1 = 2.0 * inv[rows(1)]
            d2 = 2.0 * inv[rows(2)]
            for m in range(1, 9):
                amp[which, m, rows(0)] = amp[which, m, rows(0)] * (d1 if m < 4 else d2)

        loop(channels // 16, block)

    def backward(t, g):
        which = t * 2 + g
        base = which * pairs

        def slot(p):
            ys = [twin(harm[g * pairs + p, m * 8 : (m + 1) * 8]) for m in range(8)]
            total = [jnp.zeros((16, atoms), F32) for _ in range(9)]
            lanes = pl.ds(mult(p * atoms, atoms), atoms)
            for c in range(0, channels, 16):
                rows = slice(c, c + 16)
                v = feat[base + p, rows]
                r = [rad[base + p, l * channels + c : l * channels + c + 16] for l in range(3)]
                q = [drad[base + p, l * channels + c : l * channels + c + 16] for l in range(3)]
                d = [amp[which, m, rows] for m in range(9)]
                t1 = ys[0] * d[1] + ys[1] * d[2] + ys[2] * d[3]
                t2 = ys[3] * d[4] + ys[4] * d[5] + ys[5] * d[6] + ys[6] * d[7] + ys[7] * d[8]
                if t == 1:
                    cot_feat[g, rows, lanes] = (r[0] * d[0] + r[1] * t1 + r[2] * t2).astype(BF16)
                total[0] = total[0] + v * (q[0] * d[0] + q[1] * t1 + q[2] * t2)
                p1, p2 = v * r[1], v * r[2]
                for m in range(1, 9):
                    total[m] = total[m] + (p1 if m < 4 else p2) * d[m]
            for m in range(9):
                part = total[m][:8] + total[m][8:]
                spots = pl.ds(mult(p * 8, 8), 8)
                if t == 1:
                    acc_ref[g, m, spots] = part
                else:
                    acc_ref[g, m, spots] = acc_ref[g, m, spots] + part

        loop(pairs, slot)

    start_b = start_t.astype(BF16)
    gather(0, 0, start_b, None)
    forward(0, 0)
    inv_own = inv[...]
    wait_in(0)
    gather(0, 1, start_b, recv_buf[0].T.astype(BF16))
    forward(0, 1)
    inv_both = jnp.where(low_of(inv_own), inv_own, inv[...])
    first_b = (start_t + dot(mix_t[0], split_rows(inv_both))).astype(BF16)
    send_buf[1] = dot_nt(sel[...], first_b)
    send(1, False)
    first_ref[...] = first_b.astype(F32)

    def energy(g):
        own = dup(first_ref[...], g)
        second = own + dot(mix_t[1], split_rows(inv[...]))
        act = dot(rh_t, split_rows(second))
        gate = 0.5 + 0.5 * jnp.tanh(0.5 * act)
        value = act * gate
        site = jnp.sum(rl_col * own, axis=0, keepdims=True) + jnp.sum(
            ro_col * value, axis=0, keepdims=True
        )
        dact = ro_col * gate * (1.0 + act - value)
        dsecond = dot(rh_c, split_rows(dact))
        return site, rl_col + dsecond, dot(mix_c[1], split_rows(dsecond))

    gather(1, 0, first_b, None)
    forward(1, 0)
    site_own, cot_own, dinv = energy(0)
    back_amp(1, 0, dinv)
    backward(1, 0)
    wait_in(1)
    gather(1, 1, first_ref[...].astype(BF16), recv_buf[1].T.astype(BF16))
    forward(1, 1)
    site_ghost, cot_ghost, dinv = energy(1)
    back_amp(1, 1, dinv)
    backward(1, 1)
    send_buf[2] = dot_nt(oh_ghost[atoms:], cot_feat[1])
    send(2, True)
    site_out[...] = jnp.where(low_of(site_own), site_own, site_ghost)
    cot = jnp.where(low_of(cot_own), cot_own, cot_ghost)
    cot = cot + dot_nt(cot_feat[0], oh_own[...]) + dot_nt(cot_feat[1], oh_ghost[:atoms])
    send_buf[3] = jnp.zeros((ghosts, atoms), F32)
    wait_in(2)
    back = recv_buf[2].T
    high = back.astype(BF16).astype(F32)
    parts = dot(jnp.concatenate([high, back - high], axis=0).astype(BF16), sel[...])
    cot = cot + parts[:channels] + parts[channels:]

    for g in range(2):
        back_amp(0, g, dot(mix_c[0], split_rows(dup(cot, g))))
        backward(0, g)

    sums = []
    for g in range(2):
        d = []
        for m in range(9):
            d.append(sum(acc_ref[g, m, pl.ds(j, pairs, stride=8), :] for j in range(8)))
        nx, ny, nz, over = geo[g]
        gx = ROOT3 * d[1] + ROOT15 * (ny * d[4] + nz * d[7] + nx * d[8])
        gy = ROOT3 * d[2] + ROOT15 * (nx * d[4] + nz * d[5] - ny * d[8])
        gz = ROOT3 * d[3] + ROOT15 * (ny * d[5] + nx * d[7]) + (3.0 * ROOT5) * nz * d[6]
        along = d[0] - (nx * gx + ny * gy + nz * gz) * over
        grad = [n * along + c * over for n, c in ((nx, gx), (ny, gy), (nz, gz))]
        folded = []
        for k in range(3):
            one = jnp.sum(grad[k], axis=0, keepdims=True)
            folded.append(one + turn(one))
            basis[g, 0, k * 8 : (k + 1) * 8] = -grad[k]
        sums.append(folded)
        basis[g, 0, 24:64] = jnp.zeros((40, atoms), F32)
        for p in range(pairs):
            row = basis[g, 0, pl.ds(p, 8, stride=8), :]
            high = row.astype(BF16).astype(F32)
            grad_cat[g, :, p * atoms : (p + 1) * atoms] = jnp.concatenate(
                [high, row - high], axis=0
            ).astype(BF16)
    send_buf[3, :, 0:16] = dot_nt(oh_ghost[atoms:], grad_cat[1])
    send(3, True)
    local = dot_nt(grad_cat[0], oh_own[...]) + dot_nt(grad_cat[1], oh_ghost[:atoms])
    local = local[:8] + local[8:]
    mine = jnp.concatenate(
        [jnp.where(low_of(sums[0][k]), sums[0][k], sums[1][k]) for k in range(3)], axis=0
    )
    local = local[:3] + mine
    wait_in(3)
    back = recv_buf[3].T
    back = back[:8] + back[8:16]
    high = back.astype(BF16).astype(F32)
    mid = (back - high).astype(BF16).astype(F32)
    parts = dot(jnp.concatenate([high, mid, back - high - mid], axis=0).astype(BF16), sel[...])
    force_out[...] = local + (parts[:8] + parts[8:16] + parts[16:24])[:3]
    for phase in range(4):
        wait_out(phase)


def solution(mesh):
    sizes = tuple(mesh.shape[axis] for axis in AXES)

    def body(
        species,
        send_list,
        neighbours,
        edge_vectors,
        embedding,
        radial_in,
        radial_mid,
        radial_out,
        mixing,
        read_linear,
        read_hidden,
        read_out,
    ):
        atoms = species.shape[0]
        channels = embedding.shape[1]
        slots = neighbours.shape[0]
        pairs = slots // 2
        hidden = radial_mid.shape[1]
        ghosts = plan_slabs(send_list.shape[3])[1]
        vmem = pl.BlockSpec(memory_space=pltpu.VMEM)
        smem = pl.BlockSpec(memory_space=pltpu.SMEM)
        site, forces = pl.pallas_call(
            functools.partial(kernel, sizes),
            out_shape=(
                jax.ShapeDtypeStruct((1, atoms), F32),
                jax.ShapeDtypeStruct((3, atoms), F32),
            ),
            in_specs=[vmem, smem] + [vmem] * 10,
            out_specs=(vmem, vmem),
            scratch_shapes=[
                pltpu.VMEM((2, 2, 8 * pairs, atoms), F32),
                pltpu.VMEM((2, 2, pairs, atoms), F32),
                pltpu.VMEM((2 * pairs, 64, atoms), F32),
                pltpu.VMEM((4 * pairs, 3 * channels, atoms), F32),
                pltpu.VMEM((4 * pairs, 3 * channels, atoms), F32),
                pltpu.VMEM((atoms, pairs * atoms), BF16),
                pltpu.VMEM((atoms + ghosts, pairs * atoms), BF16),
                pltpu.VMEM((4 * pairs, channels, atoms), F32),
                pltpu.VMEM((4, 9, channels, atoms), F32),
                pltpu.VMEM((3 * channels, atoms), F32),
                pltpu.VMEM((2, channels, pairs * atoms), BF16),
                pltpu.VMEM((2, 9, 8 * pairs, atoms), F32),
                pltpu.VMEM((2, 16, pairs * atoms), BF16),
                pltpu.VMEM((ghosts, atoms), BF16),
                pltpu.VMEM((2 * hidden, 32), BF16),
                pltpu.VMEM((2, hidden, 3 * hidden), BF16),
                pltpu.VMEM((2, 3 * channels, 3 * hidden), BF16),
                pltpu.VMEM((2, channels, 9 * channels), BF16),
                pltpu.VMEM((2, 3 * channels, 3 * channels), BF16),
                pltpu.VMEM((channels, atoms), F32),
                pltpu.VMEM((4, ghosts, channels), F32),
                pltpu.VMEM((4, ghosts, channels), F32),
                pltpu.SemaphoreType.DMA((4,)),
                pltpu.SemaphoreType.DMA((4,)),
            ],
            compiler_params=pltpu.CompilerParams(
                collective_id=0, has_side_effects=True, vmem_limit_bytes=56 * 1024 * 1024
            ),
        )(
            species.reshape(1, atoms),
            send_list,
            neighbours,
            edge_vectors,
            embedding,
            radial_in,
            radial_mid,
            radial_out,
            mixing,
            read_linear.reshape(1, channels),
            read_hidden.T,
            read_out.reshape(1, read_out.shape[0]),
        )
        return site.reshape(atoms), forces

    in_specs = (
        P(AXES),
        P("gx", "gy", "gz", None),
        P(None, AXES),
        P(None, None, AXES),
        P(),
        P(),
        P(),
        P(),
        P(),
        P(),
        P(),
        P(),
    )
    out_specs = (P(AXES), P(None, AXES))
    return jax.shard_map(body, mesh=mesh, in_specs=in_specs, out_specs=out_specs, check_vma=False)
```

```python
import functools
import itertools

import jax
import jax.numpy as jnp
from jax import lax
from jax.experimental import pallas as pl
from jax.experimental.pallas import tpu as pltpu
from jax.sharding import PartitionSpec as P

CUTOFF = 5.0
AXES = ("gx", "gy", "gz")
F32 = jnp.float32
BF16 = jnp.bfloat16
MESH = pl.DeviceIdType.MESH
ROOT3 = 3.0**0.5
ROOT5 = 5.0**0.5
ROOT15 = 15.0**0.5
PI = 3.141592653589793
LOAD_ORDER = (1, 0, 4, 2, 3, 5, 6, 7, 9, 8, 10, 11)


def plan_slabs(cell_rows):
    picks = {1: (1,), -1: (0,), 0: (0, 1)}
    slabs, offset = [], 0
    for count in (1, 2, 3):
        for step in itertools.product((-1, 0, 1), repeat=3):
            if sum(s != 0 for s in step) != count:
                continue
            cells = list(itertools.product(*[picks[s] for s in step]))
            if len(cells) == 1:
                cells.append(None)
            blocks = [tuple(cells[i : i + 2]) for i in range(0, len(cells), 2)]
            slabs.append((step, offset, 8 * len(blocks), blocks))
            offset += 8 * len(blocks)
    return slabs, offset


def ghost_row(step, cell, atoms, cell_rows):
    spots = [{1: 0, -1: 3, 0: c + 1}[s] for s, c in zip(step, cell)]
    return atoms + (16 * spots[0] + 4 * spots[1] + spots[2]) * cell_rows


def split_rows(x):
    high = x.astype(BF16).astype(F32)
    return jnp.concatenate([high, x - high, high], axis=0).astype(BF16)


def weight_rows(w):
    high = w.astype(BF16).astype(F32)
    return jnp.concatenate([high, high, w - high], axis=0)


def dot(a, b):
    return lax.dot_general(a, b, (((1,), (0,)), ((), ())), preferred_element_type=F32)


def dot_nt(a, b):
    return lax.dot_general(a, b, (((1,), (1,)), ((), ())), preferred_element_type=F32)


def mult(x, n):
    return x if isinstance(x, int) else pl.multiple_of(x, n)


def loop(count, body):
    for i in range(count):
        body(i)


def kernel(
    sizes,
    operands,
    site_out,
    force_out,
    basis,
    cut,
    harm,
    rad,
    drad,
    oh_own,
    oh_ghost,
    oh_edge,
    feat,
    amp,
    cot_feat,
    acc_ref,
    grad_cat,
    sel,
    sel_b,
    rep,
    w_in,
    w_mid,
    w_out,
    mix_t,
    mix_c,
    first_ref,
    send_buf,
    recv_buf,
    send_sem,
    recv_sem,
    held,
    held_sem,
):
    (
        species,
        send_list,
        neighbours,
        vectors,
        embedding,
        radial_in,
        radial_mid,
        radial_out,
        mixing,
        read_linear,
        read_hidden,
        read_out,
    ) = held
    atoms = species.shape[1]
    half = atoms // 2
    channels = embedding.shape[1]
    pairs = neighbours.shape[0] // 2
    cell_rows = send_list.shape[3]
    hidden = radial_mid.shape[1]
    slabs, ghosts = plan_slabs(cell_rows)
    me = [lax.axis_index(axis) for axis in AXES]

    def at(step):
        return tuple(
            m if s == 0 else lax.rem(m + (s + n), n) for m, s, n in zip(me, step, sizes)
        )

    barrier = pltpu.get_barrier_semaphore()
    for step, _, _, _ in slabs:
        pl.semaphore_signal(barrier, inc=1, device_id=at(step), device_id_type=MESH)

    loads = [
        pltpu.make_async_copy(source, goal, held_sem.at[i])
        for i, (source, goal) in enumerate(zip(operands, held))
    ]
    for i in LOAD_ORDER:
        loads[i].start()

    def send(phase, back):
        for step, offset, rows, _ in slabs:
            goal = tuple(-s for s in step) if back else step
            pltpu.make_async_remote_copy(
                src_ref=send_buf.at[phase, pl.ds(offset, rows)],
                dst_ref=recv_buf.at[phase, pl.ds(offset, rows)],
                send_sem=send_sem.at[phase],
                recv_sem=recv_sem.at[phase],
                device_id=at(goal),
                device_id_type=MESH,
            ).start()

    def wait_in(phase):
        whole = recv_buf.at[phase]
        pltpu.make_async_copy(whole, whole, recv_sem.at[phase]).wait()

    def wait_out(phase):
        whole = send_buf.at[phase]
        pltpu.make_async_copy(whole, whole, send_sem.at[phase]).wait()

    lane = lax.broadcasted_iota(jnp.int32, (8, atoms), 1)
    sub = lax.broadcasted_iota(jnp.int32, (8, atoms), 0)
    low8 = lane < half
    few = 8 * cell_rows
    turns = (half, half, few)
    counts = (pairs, pairs, 2 * neighbours.shape[0] * few // (2 * atoms))
    spread = 4 * pairs

    def low_of(x):
        return lax.broadcasted_iota(jnp.int32, x.shape, 1) < half

    def turn(x):
        return pltpu.roll(x, half, 1)

    def fold(x, group):
        x = x + turn(x)
        return x + pltpu.roll(x, few, 1) if group == 2 else x

    def dup(x, group):
        if group == 0:
            return jnp.where(low_of(x), x, turn(x))
        return jnp.where(low_of(x), turn(x), x)

    def paired(x):
        top, bottom = x[:pairs], x[pairs:]
        return (
            jnp.where(low8, top, turn(bottom)),
            jnp.where(low8, turn(top), bottom),
        )

    for i in LOAD_ORDER[:9]:
        loads[i].wait()

    cell_ids = {}
    spot = sub % cell_rows
    cells = list(itertools.product((0, 1), repeat=3))
    for cell in cells:
        value = jnp.full((8, atoms), send_list[cell + (0,)], jnp.int32)
        for k in range(1, cell_rows):
            value = jnp.where(spot == k, send_list[cell + (k,)], value)
        cell_ids[cell] = value
    none = jnp.full((8, atoms), -1, jnp.int32)
    cell_ids[None] = none

    def place(cell, shift):
        return none if cell is None else cells.index(cell) * cell_rows + sub - shift

    row_ids, chosen, rep_one, rep_all = [], [], [], []
    within = lane % few
    for step, offset, rows, blocks in slabs:
        for cell_a, cell_b in blocks:
            ids = jnp.where(sub < cell_rows, cell_ids[cell_a], cell_ids[cell_b])
            chosen.append(jnp.where(ids == lane, 1.0, 0.0))
            spots = jnp.where(sub < cell_rows, place(cell_a, 0), place(cell_b, cell_rows))
            rep_one.append(jnp.where(spots == lane, 1.0, 0.0))
            rep_all.append(jnp.where(spots == within, 1.0, 0.0))
            base_a = ghost_row(step, cell_a, atoms, cell_rows) + sub
            if cell_b is None:
                base_b = none
            else:
                base_b = ghost_row(step, cell_b, atoms, cell_rows) + sub - cell_rows
            row_ids.append(jnp.where(sub < cell_rows, base_a, base_b))
    sel[...] = jnp.concatenate(chosen, axis=0).astype(BF16)
    rep[0] = jnp.concatenate(rep_one, axis=0).astype(BF16)
    rep[1] = jnp.concatenate(rep_all, axis=0).astype(BF16)
    boundary = []
    for i in range(0, 8, 2):
        ids = jnp.where(sub < cell_rows, cell_ids[cells[i]], cell_ids[cells[i + 1]])
        boundary.append(jnp.where(ids == lane, 1.0, 0.0))
    sel_b[...] = jnp.concatenate(boundary * (atoms // few), axis=0).astype(BF16)

    kinds = jnp.where(sub == jnp.broadcast_to(species[...], (8, atoms)), 1.0, 0.0).astype(BF16)
    emb_t = embedding[...].astype(F32).T.astype(BF16)
    start_t = dot(emb_t, kinds)
    start_b = start_t.astype(BF16)
    start_edge = dot_nt(start_b, sel_b[...])
    send_buf[0] = dot_nt(rep[0], start_edge.astype(BF16))

    for t in range(2):
        pad = jnp.zeros((8, hidden), F32)
        w_in[t * hidden : (t + 1) * hidden] = (
            jnp.concatenate([weight_rows(radial_in[t]), pad], axis=0).T.astype(BF16)
        )
        w_mid[t] = weight_rows(radial_mid[t]).T.astype(BF16)
        w_out[t] = weight_rows(radial_out[t]).T.astype(BF16)

    nbr_f = neighbours[...].astype(F32)
    raw = jnp.concatenate([vectors[0], vectors[1], vectors[2], nbr_f], axis=0)
    raw_high = raw.astype(BF16).astype(F32)
    raw_mid = (raw - raw_high).astype(BF16).astype(F32)
    pieces = jnp.concatenate([raw_high, raw_mid, raw - raw_high - raw_mid], axis=0)
    pieces = dot_nt(pieces.astype(BF16), sel_b[...])
    depth = raw.shape[0]
    edge_raw = pieces[:depth] + pieces[depth : 2 * depth] + pieces[2 * depth :]

    def quarters(x):
        rows = counts[2]
        out = x[:rows]
        for i in range(1, atoms // few):
            out = jnp.where(lane[:rows] // few == i, x[i * rows : (i + 1) * rows], out)
        return jnp.concatenate([out, out], axis=0)

    slots = neighbours.shape[0]
    edge_parts = [quarters(edge_raw[k * slots : (k + 1) * slots]) for k in range(4)]
    vec = [paired(vectors[k]) + (edge_parts[k],) for k in range(3)]
    nbr = paired(nbr_f) + (edge_parts[3],)
    geo = []
    for g in range(3):
        x, y, z = vec[0][g], vec[1][g], vec[2][g]
        length = jnp.sqrt(x * x + y * y + z * z)
        over = 1.0 / length
        nx, ny, nz = x * over, y * over, z * over
        geo.append((nx, ny, nz, over))
        u = length * (1.0 / CUTOFF)
        u2 = u * u
        u4 = u2 * u2
        u5 = u4 * u
        inside = u < 1.0
        env = 1.0 - 21.0 * u5 + 35.0 * u5 * u - 15.0 * u5 * u2
        denv = (-105.0 / CUTOFF) * u4 * (1.0 - u) * (1.0 - u)
        cut[g, 0] = jnp.where(inside, 0.25 * env, 0.0)
        cut[g, 1] = jnp.where(inside, 0.25 * denv, 0.0)
        theta = PI * u
        sin1, cos1 = jnp.sin(theta), jnp.cos(theta)
        twice = 2.0 * cos1
        s_old, s_now = jnp.zeros_like(sin1), sin1
        c_old, c_now = jnp.ones_like(cos1), cos1
        amp0 = (2.0 / CUTOFF) ** 0.5
        for k in range(1, 9):
            base = amp0 * s_now * over
            slope = (amp0 * k * PI / CUTOFF * c_now - base) * over
            basis[g, 0, (k - 1) * 8 : k * 8] = base
            basis[g, 1, (k - 1) * 8 : k * 8] = slope
            s_old, s_now = s_now, twice * s_now - s_old
            c_old, c_now = c_now, twice * c_now - c_old
        ylm = (
            ROOT3 * nx,
            ROOT3 * ny,
            ROOT3 * nz,
            ROOT15 * nx * ny,
            ROOT15 * ny * nz,
            0.5 * ROOT5 * (3.0 * nz * nz - 1.0),
            ROOT15 * nx * nz,
            0.5 * ROOT15 * (nx * nx - ny * ny),
        )
        for m in range(8):
            for p in range(counts[g]):
                harm[g * pairs + p, m * 8 : (m + 1) * 8] = jnp.broadcast_to(
                    ylm[m][p : p + 1], (8, atoms)
                )

    own_rows = jnp.concatenate([sub + 8 * b for b in range(atoms // 8)], axis=0).astype(F32)
    all_rows = jnp.concatenate([own_rows] + [r.astype(F32) for r in row_ids], axis=0)
    onehots = (oh_own, oh_ghost, oh_edge)

    def onehot(g):
        ids = own_rows if g == 0 else all_rows
        for p in range(counts[g]):
            onehots[g][:, p * atoms : (p + 1) * atoms] = jnp.where(
                ids == nbr[g][p : p + 1], 1.0, 0.0
            ).astype(BF16)

    def silu_pair(x, dx):
        gate = 0.5 + 0.5 * jnp.tanh(0.5 * x)
        value = x * gate
        return value, gate * (1.0 + x - value) * dx

    def tiles(t, g):
        return spread if g == 2 else (t * 2 + g) * pairs

    def radial(g, layers):
        top = layers[-1] * hidden + hidden

        def chunk(j):
            def wide(kind):
                return jnp.concatenate(
                    [basis[g, kind, pl.ds(2 * j + i, 8, stride=8), :] for i in range(2)], axis=1
                )

            def row(kind):
                return jnp.concatenate(
                    [cut[g, kind, 2 * j + i : 2 * j + i + 1, :] for i in range(2)], axis=1
                )

            env, denv = row(0), row(1)

            def first_dot(x):
                high = x.astype(BF16).astype(F32)
                full = jnp.concatenate([high, x - high, high, jnp.zeros_like(x)], axis=0)
                return dot(w_in[:top], full.astype(BF16))

            one, done = silu_pair(first_dot(wide(0)), first_dot(wide(1)))
            for t in layers:
                rows = slice(t * hidden, (t + 1) * hidden)
                two, dtwo = silu_pair(
                    dot(w_mid[t], split_rows(one[rows])), dot(w_mid[t], split_rows(done[rows]))
                )
                value = dot(w_out[t], split_rows(env * two))
                slope = dot(w_out[t], split_rows(denv * two + env * dtwo))
                for i in range(2):
                    lanes = slice(i * atoms, (i + 1) * atoms)
                    rad[tiles(t, g) + 2 * j + i] = value[:, lanes]
                    drad[tiles(t, g) + 2 * j + i] = slope[:, lanes]

        loop(counts[g] // 2, chunk)

    def gather(t, g, own_t, ghost_t):
        for j in range(counts[g] // 2):
            lanes = slice(j * 2 * atoms, (j + 1) * 2 * atoms)
            out = dot(own_t, onehots[g][:atoms, lanes])
            if g > 0:
                out = out + dot(ghost_t, onehots[g][atoms:, lanes])
            feat[tiles(t, g) + 2 * j] = out[:, :atoms]
            feat[tiles(t, g) + 2 * j + 1] = out[:, atoms:]

    def twin(y):
        return jnp.concatenate([y, y], axis=0)

    def forward(t, g):
        which = 4 if g == 2 else t * 2 + g
        base = tiles(t, g)
        parts_out = ([], [], [])
        for c in range(0, channels, 16):
            total = [jnp.zeros((16, atoms), F32) for _ in range(9)]
            for p in range(counts[g]):
                v = feat[base + p, c : c + 16]
                parts = [
                    rad[base + p, l * channels + c : l * channels + c + 16] * v for l in range(3)
                ]
                total[0] = total[0] + parts[0]
                for m in range(8):
                    y = twin(harm[g * pairs + p, m * 8 : (m + 1) * 8])
                    total[1 + m] = total[1 + m] + y * parts[1 if m < 3 else 2]
            total = [fold(a, g) for a in total]
            for m in range(1, 9):
                amp[which, m, c : c + 16] = total[m]
            parts_out[0].append(total[0])
            parts_out[1].append(sum(a * a for a in total[1:4]))
            parts_out[2].append(sum(a * a for a in total[4:9]))
        return jnp.concatenate(parts_out[0] + parts_out[1] + parts_out[2], axis=0)

    def backward(t, g, dinv, adding):
        which = 4 if g == 2 else t * 2 + g
        base = tiles(t, g)
        for c in range(0, channels, 16):
            rows = slice(c, c + 16)
            amp[which, 0, rows] = dinv[rows]
            d1 = 2.0 * dinv[channels + c : channels + c + 16]
            d2 = 2.0 * dinv[2 * channels + c : 2 * channels + c + 16]
            for m in range(1, 9):
                amp[which, m, rows] = amp[which, m, rows] * (d1 if m < 4 else d2)
        for p in range(counts[g]):
            ys = [twin(harm[g * pairs + p, m * 8 : (m + 1) * 8]) for m in range(8)]
            total = [jnp.zeros((16, atoms), F32) for _ in range(9)]
            for c in range(0, channels, 16):
                rows = slice(c, c + 16)
                v = feat[base + p, rows]
                r = [rad[base + p, l * channels + c : l * channels + c + 16] for l in range(3)]
                q = [drad[base + p, l * channels + c : l * channels + c + 16] for l in range(3)]
                d = [amp[which, m, rows] for m in range(9)]
                t1 = ys[0] * d[1] + ys[1] * d[2] + ys[2] * d[3]
                t2 = ys[3] * d[4] + ys[4] * d[5] + ys[5] * d[6] + ys[6] * d[7] + ys[7] * d[8]
                if t == 1:
                    cot_feat[g, rows, p * atoms : (p + 1) * atoms] = (
                        r[0] * d[0] + r[1] * t1 + r[2] * t2
                    ).astype(BF16)
                total[0] = total[0] + v * (q[0] * d[0] + q[1] * t1 + q[2] * t2)
                p1, p2 = v * r[1], v * r[2]
                for m in range(1, 9):
                    total[m] = total[m] + (p1 if m < 4 else p2) * d[m]
            for m in range(9):
                part = total[m][:8] + total[m][8:]
                spots = slice(p * 8, (p + 1) * 8)
                if adding:
                    part = part + acc_ref[g, m, spots]
                acc_ref[g, m, spots] = part

    def edge_grads(g):
        n = counts[g]
        d = []
        for m in range(9):
            d.append(sum(acc_ref[g, m, pl.ds(j, n, stride=8), :] for j in range(8)))
        nx, ny, nz, over = [v[:n] for v in geo[g]]
        gx = ROOT3 * d[1] + ROOT15 * (ny * d[4] + nz * d[7] + nx * d[8])
        gy = ROOT3 * d[2] + ROOT15 * (nx * d[4] + nz * d[5] - ny * d[8])
        gz = ROOT3 * d[3] + ROOT15 * (ny * d[5] + nx * d[7]) + (3.0 * ROOT5) * nz * d[6]
        along = d[0] - (nx * gx + ny * gy + nz * gz) * over
        grad = [a * along + b * over for a, b in ((nx, gx), (ny, gy), (nz, gz))]
        basis[g, 0, 0:64] = jnp.zeros((64, atoms), F32)
        for k in range(3):
            basis[g, 0, k * 8 : k * 8 + n] = -grad[k]
        for p in range(n):
            row = basis[g, 0, pl.ds(p, 8, stride=8), :]
            high = row.astype(BF16).astype(F32)
            grad_cat[g, :, p * atoms : (p + 1) * atoms] = jnp.concatenate(
                [high, row - high], axis=0
            ).astype(BF16)
        return [fold(jnp.sum(v, axis=0, keepdims=True), g) for v in grad]

    onehot(2)
    radial(2, (0,))
    onehot(0)
    onehot(1)
    radial(0, (0, 1))
    pl.semaphore_wait(barrier, len(slabs))
    send(0, False)
    radial(1, (0, 1))
    for i in LOAD_ORDER[9:]:
        loads[i].wait()
    mix_t[...] = weight_rows(mixing[0]).T.astype(BF16)
    high = mixing[0].astype(BF16).astype(F32)
    mix_c[...] = jnp.concatenate([high, high, mixing[0] - high], axis=1).astype(BF16)
    rl_col = jnp.broadcast_to(read_linear[...], (channels, channels)).T
    rh = read_hidden[...]
    rh_high = rh.astype(BF16).astype(F32)
    rh_two = jnp.concatenate([rh_high, rh - rh_high], axis=1).astype(BF16)
    rh_t = jnp.concatenate([rh_high, rh_high, rh - rh_high], axis=1).astype(BF16)
    rh_c = weight_rows(rh).T.astype(BF16)
    ro_col = jnp.broadcast_to(read_out[...], (channels, read_out.shape[1])).T
    high = mixing[1].astype(BF16).astype(F32)
    mixed = dot_nt(
        rh_t, jnp.concatenate([high, mixing[1] - high, high], axis=1).astype(BF16)
    )
    high = mixed.astype(BF16).astype(F32)
    act_w = jnp.concatenate([high, high, mixed - high], axis=1).astype(BF16)
    dact_w = weight_rows(mixed).T.astype(BF16)
    gather(0, 0, start_b, None)
    inv_own = forward(0, 0)

    wait_in(0)
    ghost_t = recv_buf[0].T.astype(BF16)
    gather(0, 2, start_b, ghost_t)
    first_edge = start_edge + dot(mix_t[...], split_rows(forward(0, 2)))
    send_buf[1] = dot_nt(rep[0], first_edge.astype(BF16))
    send(1, False)
    gather(0, 1, start_b, ghost_t)
    inv_both = jnp.where(low_of(inv_own), inv_own, forward(0, 1))
    first_b = (start_t + dot(mix_t[...], split_rows(inv_both))).astype(BF16)
    first_ref[...] = first_b.astype(F32)

    def energy_own(g):
        own = dup(first_ref[...], g)
        doubled = jnp.concatenate([own, own], axis=0).astype(BF16)
        return jnp.sum(rl_col * own, axis=0, keepdims=True), dot(rh_two, doubled)

    def energy(features, site, act):
        act = act + dot(act_w, split_rows(features))
        gate = 0.5 + 0.5 * jnp.tanh(0.5 * act)
        value = act * gate
        site = site + jnp.sum(ro_col * value, axis=0, keepdims=True)
        dact = split_rows(ro_col * gate * (1.0 + act - value))
        return site, dact, dot(dact_w, dact)

    gather(1, 0, first_b, None)
    site_own, dact_own, dinv = energy(forward(1, 0), *energy_own(0))
    backward(1, 0, dinv, False)
    before = energy_own(1)
    wait_in(1)
    gather(1, 1, first_b, recv_buf[1].T.astype(BF16))
    site_ghost, dact_ghost, dinv = energy(forward(1, 1), *before)
    backward(1, 1, dinv, False)
    send_buf[2] = dot_nt(oh_ghost[atoms:], cot_feat[1])
    send(2, True)
    site_out[...] = jnp.where(low_of(site_own), site_own, site_ghost)

    cot_own, cot_ghost = dot(rh_c, dact_own), dot(rh_c, dact_ghost)
    cot = rl_col + jnp.where(low_of(cot_own), cot_own, cot_ghost)
    cot = cot + dot_nt(cot_feat[0], oh_own[...]) + dot_nt(cot_feat[1], oh_ghost[:atoms])
    sums = []
    for g in range(2):
        backward(0, g, dot(mix_c[...], split_rows(dup(cot, g))), True)
        sums.append(edge_grads(g))
    outward = dot_nt(oh_ghost[atoms:], grad_cat[1])
    local = dot_nt(grad_cat[0], oh_own[...]) + dot_nt(grad_cat[1], oh_ghost[:atoms])
    mine = jnp.concatenate(
        [jnp.where(low_of(sums[0][k]), sums[0][k], sums[1][k]) for k in range(3)], axis=0
    )
    local = local[:3] + local[8:11] + mine
    send_buf[3] = jnp.zeros((ghosts, atoms), F32)

    wait_in(2)
    back = recv_buf[2].T
    high = back.astype(BF16).astype(F32)
    parts = dot(jnp.concatenate([high, back - high], axis=0).astype(BF16), rep[1])
    dinv = dot(mix_c[...], split_rows(parts[:channels] + parts[channels:]))
    backward(0, 2, dinv, False)
    sums = edge_grads(2)
    width = counts[2] * atoms
    send_buf[3, :, 0:16] = outward + dot_nt(oh_edge[atoms:], grad_cat[2, :, :width])
    send(3, True)
    parts = dot_nt(grad_cat[2, :, :width], oh_edge[:atoms])
    local = local + parts[:3] + parts[8:11]
    rows = jnp.concatenate(sums + [jnp.zeros((5, atoms), F32)], axis=0)
    rows = jnp.where(lane < few, rows, 0.0)

    def exact(x, chooser):
        high = x.astype(BF16).astype(F32)
        mid = (x - high).astype(BF16).astype(F32)
        out = dot(jnp.concatenate([high, mid, x - high - mid], axis=0).astype(BF16), chooser)
        return out[:3] + out[8:11] + out[16:19]

    local = local + exact(rows, sel_b[...])
    wait_in(3)
    back = recv_buf[3].T
    force_out[...] = local + exact(back[:8] + back[8:16], sel[...])
    for phase in range(4):
        wait_out(phase)


def finish(site_in, force_in, site_out, force_out):
    site_out[...] = site_in[0]
    force_out[...] = force_in[...]


def solution(mesh):
    sizes = tuple(mesh.shape[axis] for axis in AXES)

    def body(
        species,
        send_list,
        neighbours,
        edge_vectors,
        embedding,
        radial_in,
        radial_mid,
        radial_out,
        mixing,
        read_linear,
        read_hidden,
        read_out,
    ):
        atoms = species.shape[0]
        channels = embedding.shape[1]
        slots = neighbours.shape[0]
        pairs = slots // 2
        hidden = radial_mid.shape[1]
        ghosts = plan_slabs(send_list.shape[3])[1]
        vmem = pl.BlockSpec(memory_space=pltpu.VMEM)
        operands = (
            species.reshape(1, atoms),
            send_list,
            neighbours,
            edge_vectors,
            embedding,
            radial_in,
            radial_mid,
            radial_out,
            mixing,
            read_linear.reshape(1, channels),
            read_hidden.T,
            read_out.reshape(1, read_out.shape[0]),
        )
        site, forces = pl.pallas_call(
            functools.partial(kernel, sizes),
            out_shape=(pltpu.VMEM((1, atoms), F32), pltpu.VMEM((3, atoms), F32)),
            in_specs=[tuple(pl.BlockSpec(memory_space=pltpu.HBM) for _ in operands)],
            out_specs=(vmem, vmem),
            scratch_shapes=[
                pltpu.VMEM((3, 2, 8 * pairs, atoms), F32),
                pltpu.VMEM((3, 2, pairs, atoms), F32),
                pltpu.VMEM((3 * pairs, 64, atoms), F32),
                pltpu.VMEM((5 * pairs, 3 * channels, atoms), F32),
                pltpu.VMEM((5 * pairs, 3 * channels, atoms), F32),
                pltpu.VMEM((atoms, pairs * atoms), BF16),
                pltpu.VMEM((atoms + ghosts, pairs * atoms), BF16),
                pltpu.VMEM((atoms + ghosts, pairs * atoms // 2), BF16),
                pltpu.VMEM((5 * pairs, channels, atoms), F32),
                pltpu.VMEM((5, 9, channels, atoms), F32),
                pltpu.VMEM((2, channels, pairs * atoms), BF16),
                pltpu.VMEM((3, 9, 8 * pairs, atoms), F32),
                pltpu.VMEM((3, 16, pairs * atoms), BF16),
                pltpu.VMEM((ghosts, atoms), BF16),
                pltpu.VMEM((atoms, atoms), BF16),
                pltpu.VMEM((2, ghosts, atoms), BF16),
                pltpu.VMEM((2 * hidden, 32), BF16),
                pltpu.VMEM((2, hidden, 3 * hidden), BF16),
                pltpu.VMEM((2, 3 * channels, 3 * hidden), BF16),
                pltpu.VMEM((channels, 9 * channels), BF16),
                pltpu.VMEM((3 * channels, 3 * channels), BF16),
                pltpu.VMEM((channels, atoms), F32),
                pltpu.VMEM((4, ghosts, channels), F32),
                pltpu.VMEM((4, ghosts, channels), F32),
                pltpu.SemaphoreType.DMA((4,)),
                pltpu.SemaphoreType.DMA((4,)),
                tuple(
                    (pltpu.SMEM if x is send_list else pltpu.VMEM)(x.shape, x.dtype)
                    for x in operands
                ),
                pltpu.SemaphoreType.DMA((len(operands),)),
            ],
            compiler_params=pltpu.CompilerParams(
                collective_id=0, has_side_effects=True, vmem_limit_bytes=56 * 1024 * 1024
            ),
        )(operands)
        site, forces = [pltpu.with_memory_space_constraint(x, pltpu.VMEM) for x in (site, forces)]
        return pl.pallas_call(
            finish,
            out_shape=(
                jax.ShapeDtypeStruct((atoms,), F32),
                jax.ShapeDtypeStruct((3, atoms), F32),
            ),
            in_specs=[vmem, vmem],
            out_specs=(vmem, vmem),
        )(site, forces)

    in_specs = (
        P(AXES),
        P("gx", "gy", "gz", None),
        P(None, AXES),
        P(None, None, AXES),
        P(),
        P(),
        P(),
        P(),
        P(),
        P(),
        P(),
        P(),
    )
    out_specs = (P(AXES), P(None, AXES))
    return jax.shard_map(body, mesh=mesh, in_specs=in_specs, out_specs=out_specs, check_vma=False)
```

```python
import functools
import itertools

import jax
import jax.numpy as jnp
from jax import lax
from jax.experimental import pallas as pl
from jax.experimental.pallas import tpu as pltpu
from jax.sharding import PartitionSpec as P

CUTOFF = 5.0
AXES = ("gx", "gy", "gz")
F32 = jnp.float32
BF16 = jnp.bfloat16
MESH = pl.DeviceIdType.MESH
ROOT3 = 3.0**0.5
ROOT5 = 5.0**0.5
ROOT15 = 15.0**0.5
PI = 3.141592653589793
WIDE = 8
LOAD_ORDER = (1, 0, 4, 2, 3, 5, 6, 7, 9, 8, 10, 11)


def plan_slabs(cell_rows):
    picks = {1: (1,), -1: (0,), 0: (0, 1)}
    slabs, offset = [], 0
    for count in (1, 2, 3):
        for step in itertools.product((-1, 0, 1), repeat=3):
            if sum(s != 0 for s in step) != count:
                continue
            cells = list(itertools.product(*[picks[s] for s in step]))
            if len(cells) == 1:
                cells.append(None)
            blocks = [tuple(cells[i : i + 2]) for i in range(0, len(cells), 2)]
            slabs.append((step, offset, 8 * len(blocks), blocks))
            offset += 8 * len(blocks)
    return slabs, offset


def ghost_row(step, cell, atoms, cell_rows):
    spots = [{1: 0, -1: 3, 0: c + 1}[s] for s, c in zip(step, cell)]
    return atoms + (16 * spots[0] + 4 * spots[1] + spots[2]) * cell_rows


def split_rows(x):
    high = x.astype(BF16).astype(F32)
    return jnp.concatenate([high, x - high, high], axis=0).astype(BF16)


def weight_rows(w):
    high = w.astype(BF16).astype(F32)
    return jnp.concatenate([high, high, w - high], axis=0)


def dot(a, b):
    return lax.dot_general(a, b, (((1,), (0,)), ((), ())), preferred_element_type=F32)


def dot_nt(a, b):
    return lax.dot_general(a, b, (((1,), (1,)), ((), ())), preferred_element_type=F32)


def mult(x, n):
    return x if isinstance(x, int) else pl.multiple_of(x, n)


def loop(count, body):
    for i in range(count):
        body(i)


def kernel(
    sizes,
    operands,
    site_out,
    force_out,
    basis,
    cut,
    harm,
    rad,
    drad,
    oh_own,
    oh_ghost,
    oh_edge,
    feat,
    amp,
    cot_feat,
    acc_ref,
    grad_cat,
    sel,
    sel_b,
    rep,
    w_in,
    w_mid,
    w_out,
    mix_t,
    mix_c,
    first_ref,
    send_buf,
    recv_buf,
    send_sem,
    recv_sem,
    part,
    edge_jac,
    held,
    held_sem,
):
    (
        species,
        send_list,
        neighbours,
        vectors,
        embedding,
        radial_in,
        radial_mid,
        radial_out,
        mixing,
        read_linear,
        read_hidden,
        read_out,
    ) = held
    atoms = species.shape[1]
    half = atoms // 2
    channels = embedding.shape[1]
    pairs = neighbours.shape[0] // 2
    cell_rows = send_list.shape[3]
    hidden = radial_mid.shape[1]
    slabs, ghosts = plan_slabs(cell_rows)
    ways = []
    for step, _, _, _ in slabs:
        kind = sum(s != 0 for s in step) - 1
        ways.append((kind, sum(way[0] == kind for way in ways), step))
    me = [lax.axis_index(axis) for axis in AXES]

    def at(step):
        return tuple(
            m if s == 0 else lax.rem(m + (s + n), n) for m, s, n in zip(me, step, sizes)
        )

    barrier = pltpu.get_barrier_semaphore()
    for step, _, _, _ in slabs:
        pl.semaphore_signal(barrier, inc=1, device_id=at(step), device_id_type=MESH)

    loads = [
        pltpu.make_async_copy(source, goal, held_sem.at[i])
        for i, (source, goal) in enumerate(zip(operands, held))
    ]
    for i in LOAD_ORDER:
        loads[i].start()

    def send(phase, back):
        for kind, index, step in ways:
            goal = tuple(-s for s in step) if back else step
            pltpu.make_async_remote_copy(
                src_ref=send_buf[kind].at[phase, index],
                dst_ref=recv_buf[kind].at[phase, index],
                send_sem=send_sem.at[phase, kind],
                recv_sem=recv_sem.at[phase, kind],
                device_id=at(goal),
                device_id_type=MESH,
            ).start()

    def wait_all(bufs, sems, phase):
        for kind, buf in enumerate(bufs):
            whole = buf.at[phase]
            pltpu.make_async_copy(whole, whole, sems.at[phase, kind]).wait()

    def wait_in(phase):
        wait_all(recv_buf, recv_sem, phase)

    def wait_out(phase):
        wait_all(send_buf, send_sem, phase)

    def fill(phase, rows):
        start = 0
        for buf in send_buf:
            count, depth = buf.shape[1:3]
            part_rows = rows[start : start + count * depth]
            buf[phase, :, :, : rows.shape[1]] = part_rows.reshape(
                count, depth, rows.shape[1]
            ).astype(BF16)
            start += count * depth

    def arrived(phase):
        parts = []
        for buf in recv_buf:
            block = buf[phase]
            count, depth, width = block.shape
            if depth % 16:
                block = block.astype(F32).reshape(count * depth, width).astype(BF16)
            parts.append(block.reshape(count * depth, width))
        return jnp.concatenate(parts, axis=0).T

    lane = lax.broadcasted_iota(jnp.int32, (8, atoms), 1)
    sub = lax.broadcasted_iota(jnp.int32, (8, atoms), 0)
    low8 = lane < half
    few = 8 * cell_rows
    turns = (half, half, few)
    counts = (pairs, pairs, 2 * neighbours.shape[0] * few // (2 * atoms))
    spread = 4 * pairs

    def low_of(x):
        return lax.broadcasted_iota(jnp.int32, x.shape, 1) < half

    def turn(x):
        return pltpu.roll(x, half, 1)

    def fold(x, group):
        x = x + turn(x)
        return x + pltpu.roll(x, few, 1) if group == 2 else x

    def dup(x, group):
        if group == 0:
            return jnp.where(low_of(x), x, turn(x))
        return jnp.where(low_of(x), turn(x), x)

    def paired(x):
        top, bottom = x[:pairs], x[pairs:]
        return (
            jnp.where(low8, top, turn(bottom)),
            jnp.where(low8, turn(top), bottom),
        )

    for i in LOAD_ORDER:
        loads[i].wait()

    cell_ids = {}
    spot = sub % cell_rows
    cells = list(itertools.product((0, 1), repeat=3))
    for cell in cells:
        value = jnp.full((8, atoms), send_list[cell + (0,)], jnp.int32)
        for k in range(1, cell_rows):
            value = jnp.where(spot == k, send_list[cell + (k,)], value)
        cell_ids[cell] = value
    none = jnp.full((8, atoms), -1, jnp.int32)
    cell_ids[None] = none

    def place(cell, shift):
        return none if cell is None else cells.index(cell) * cell_rows + sub - shift

    row_ids, chosen, rep_one, rep_all = [], [], [], []
    within = lane % few
    for step, offset, rows, blocks in slabs:
        for cell_a, cell_b in blocks:
            ids = jnp.where(sub < cell_rows, cell_ids[cell_a], cell_ids[cell_b])
            chosen.append(jnp.where(ids == lane, 1.0, 0.0))
            spots = jnp.where(sub < cell_rows, place(cell_a, 0), place(cell_b, cell_rows))
            rep_one.append(jnp.where(spots == lane, 1.0, 0.0))
            rep_all.append(jnp.where(spots == within, 1.0, 0.0))
            base_a = ghost_row(step, cell_a, atoms, cell_rows) + sub
            if cell_b is None:
                base_b = none
            else:
                base_b = ghost_row(step, cell_b, atoms, cell_rows) + sub - cell_rows
            row_ids.append(jnp.where(sub < cell_rows, base_a, base_b))
    sel[...] = jnp.concatenate(chosen, axis=0).astype(BF16)
    rep[0] = jnp.concatenate(rep_one, axis=0).astype(BF16)
    rep[1] = jnp.concatenate(rep_all, axis=0).astype(BF16)
    boundary = []
    for i in range(0, 8, 2):
        ids = jnp.where(sub < cell_rows, cell_ids[cells[i]], cell_ids[cells[i + 1]])
        boundary.append(jnp.where(ids == lane, 1.0, 0.0))
    sel_b[...] = jnp.concatenate(boundary * (atoms // few), axis=0).astype(BF16)

    kinds = jnp.where(sub == jnp.broadcast_to(species[...], (8, atoms)), 1.0, 0.0).astype(BF16)
    emb_t = embedding[...].astype(F32).T.astype(BF16)
    start_t = dot(emb_t, kinds)
    start_b = start_t.astype(BF16)
    start_edge = dot_nt(start_b, sel_b[...])
    fill(0, dot_nt(rep[0], start_edge.astype(BF16)))

    for t in range(2):
        pad = jnp.zeros((8, hidden), F32)
        w_in[t * hidden : (t + 1) * hidden] = (
            jnp.concatenate([weight_rows(radial_in[t]), pad], axis=0).T.astype(BF16)
        )
        w_mid[t] = weight_rows(radial_mid[t]).T.astype(BF16)
        w_out[t] = weight_rows(radial_out[t]).T.astype(BF16)

    nbr_f = neighbours[...].astype(F32)
    raw = jnp.concatenate([vectors[0], vectors[1], vectors[2], nbr_f], axis=0)
    raw_high = raw.astype(BF16).astype(F32)
    raw_mid = (raw - raw_high).astype(BF16).astype(F32)
    pieces = jnp.concatenate([raw_high, raw_mid, raw - raw_high - raw_mid], axis=0)
    pieces = dot_nt(pieces.astype(BF16), sel_b[...])
    depth = raw.shape[0]
    edge_raw = pieces[:depth] + pieces[depth : 2 * depth] + pieces[2 * depth :]

    def quarters(x):
        rows = counts[2]
        out = x[:rows]
        for i in range(1, atoms // few):
            out = jnp.where(lane[:rows] // few == i, x[i * rows : (i + 1) * rows], out)
        return jnp.concatenate([out, out], axis=0)

    slots = neighbours.shape[0]
    edge_parts = [quarters(edge_raw[k * slots : (k + 1) * slots]) for k in range(4)]
    vec = [paired(vectors[k]) + (edge_parts[k],) for k in range(3)]
    nbr = paired(nbr_f) + (edge_parts[3],)
    geo = []
    for g in range(3):
        x, y, z = vec[0][g], vec[1][g], vec[2][g]
        length = jnp.sqrt(x * x + y * y + z * z)
        over = 1.0 / length
        nx, ny, nz = x * over, y * over, z * over
        geo.append((nx, ny, nz, over))
        u = length * (1.0 / CUTOFF)
        u2 = u * u
        u4 = u2 * u2
        u5 = u4 * u
        inside = u < 1.0
        env = 1.0 - 21.0 * u5 + 35.0 * u5 * u - 15.0 * u5 * u2
        denv = (-105.0 / CUTOFF) * u4 * (1.0 - u) * (1.0 - u)
        cut[g, 0] = jnp.where(inside, 0.25 * env, 0.0)
        cut[g, 1] = jnp.where(inside, 0.25 * denv, 0.0)
        theta = PI * u
        sin1, cos1 = jnp.sin(theta), jnp.cos(theta)
        twice = 2.0 * cos1
        s_old, s_now = jnp.zeros_like(sin1), sin1
        c_old, c_now = jnp.ones_like(cos1), cos1
        amp0 = (2.0 / CUTOFF) ** 0.5
        for k in range(1, 9):
            base = amp0 * s_now * over
            slope = (amp0 * k * PI / CUTOFF * c_now - base) * over
            basis[g, 0, (k - 1) * 8 : k * 8] = base
            basis[g, 1, (k - 1) * 8 : k * 8] = slope
            s_old, s_now = s_now, twice * s_now - s_old
            c_old, c_now = c_now, twice * c_now - c_old
        ylm = (
            ROOT3 * nx,
            ROOT3 * ny,
            ROOT3 * nz,
            ROOT15 * nx * ny,
            ROOT15 * ny * nz,
            0.5 * ROOT5 * (3.0 * nz * nz - 1.0),
            ROOT15 * nx * nz,
            0.5 * ROOT15 * (nx * nx - ny * ny),
        )
        for m in range(8):
            for p in range(counts[g]):
                harm[g * pairs + p, m * 8 : (m + 1) * 8] = jnp.broadcast_to(
                    ylm[m][p : p + 1], (8, atoms)
                )

    own_rows = jnp.concatenate([sub + 8 * b for b in range(atoms // 8)], axis=0).astype(F32)
    all_rows = jnp.concatenate([own_rows] + [r.astype(F32) for r in row_ids], axis=0)
    onehots = (oh_own, oh_ghost, oh_edge)

    def onehot(g):
        ids = own_rows if g == 0 else all_rows
        for p in range(counts[g]):
            onehots[g][:, p * atoms : (p + 1) * atoms] = jnp.where(
                ids == nbr[g][p : p + 1], 1.0, 0.0
            ).astype(BF16)

    def silu_pair(x, dx):
        gate = 0.5 + 0.5 * jnp.tanh(0.5 * x)
        value = x * gate
        return value, gate * (1.0 + x - value) * dx

    def tiles(t, g):
        return spread if g == 2 else (t * 2 + g) * pairs

    def radial(g, layers):
        top = layers[-1] * hidden + hidden

        def chunk(j):
            spots = range(j * WIDE, min(counts[g], (j + 1) * WIDE))

            def wide(kind):
                return jnp.concatenate(
                    [basis[g, kind, pl.ds(p, 8, stride=8), :] for p in spots], axis=1
                )

            def row(kind):
                return jnp.concatenate([cut[g, kind, p : p + 1, :] for p in spots], axis=1)

            env, denv = row(0), row(1)

            def first_dot(x):
                high = x.astype(BF16).astype(F32)
                full = jnp.concatenate([high, x - high, high, jnp.zeros_like(x)], axis=0)
                return dot(w_in[:top], full.astype(BF16))

            one, done = silu_pair(first_dot(wide(0)), first_dot(wide(1)))
            for t in layers:
                rows = slice(t * hidden, (t + 1) * hidden)
                two, dtwo = silu_pair(
                    dot(w_mid[t], split_rows(one[rows])), dot(w_mid[t], split_rows(done[rows]))
                )
                value = dot(w_out[t], split_rows(env * two))
                slope = dot(w_out[t], split_rows(denv * two + env * dtwo))
                for i, p in enumerate(spots):
                    lanes = slice(i * atoms, (i + 1) * atoms)
                    rad[tiles(t, g) + p] = value[:, lanes]
                    drad[tiles(t, g) + p] = slope[:, lanes]

        loop(-(-counts[g] // WIDE), chunk)

    def gather(t, g, rows_t, ghosts_too=False):
        for j in range(counts[g] // 2):
            lanes = slice(j * 2 * atoms, (j + 1) * 2 * atoms)
            first, second = tiles(t, g) + 2 * j, tiles(t, g) + 2 * j + 1
            if ghosts_too:
                out = dot(rows_t, onehots[g][atoms:, lanes])
                feat[first] = feat[first] + out[:, :atoms]
                feat[second] = feat[second] + out[:, atoms:]
            else:
                out = dot(rows_t, onehots[g][:atoms, lanes])
                feat[first] = out[:, :atoms]
                feat[second] = out[:, atoms:]

    def twin(y):
        return jnp.concatenate([y, y], axis=0)

    def forward(t, g):
        which = 4 if g == 2 else t * 2 + g
        base = tiles(t, g)
        parts_out = ([], [], [])
        for c in range(0, channels, 16):
            total = [jnp.zeros((16, atoms), F32) for _ in range(9)]
            for p in range(counts[g]):
                v = feat[base + p, c : c + 16]
                parts = [
                    rad[base + p, l * channels + c : l * channels + c + 16] * v for l in range(3)
                ]
                total[0] = total[0] + parts[0]
                for m in range(8):
                    y = twin(harm[g * pairs + p, m * 8 : (m + 1) * 8])
                    total[1 + m] = total[1 + m] + y * parts[1 if m < 3 else 2]
            total = [fold(a, g) for a in total]
            for m in range(1, 9):
                amp[which, m, c : c + 16] = total[m]
            parts_out[0].append(total[0])
            parts_out[1].append(sum(a * a for a in total[1:4]))
            parts_out[2].append(sum(a * a for a in total[4:9]))
        return jnp.concatenate(parts_out[0] + parts_out[1] + parts_out[2], axis=0)

    def backward(t, g, dinv, adding):
        which = 4 if g == 2 else t * 2 + g
        base = tiles(t, g)
        for c in range(0, channels, 16):
            rows = slice(c, c + 16)
            amp[which, 0, rows] = dinv[rows]
            d1 = 2.0 * dinv[channels + c : channels + c + 16]
            d2 = 2.0 * dinv[2 * channels + c : 2 * channels + c + 16]
            for m in range(1, 9):
                amp[which, m, rows] = amp[which, m, rows] * (d1 if m < 4 else d2)
        for p in range(counts[g]):
            ys = [twin(harm[g * pairs + p, m * 8 : (m + 1) * 8]) for m in range(8)]
            total = [jnp.zeros((16, atoms), F32) for _ in range(9)]
            for c in range(0, channels, 16):
                rows = slice(c, c + 16)
                v = feat[base + p, rows]
                r = [rad[base + p, l * channels + c : l * channels + c + 16] for l in range(3)]
                q = [drad[base + p, l * channels + c : l * channels + c + 16] for l in range(3)]
                d = [amp[which, m, rows] for m in range(9)]
                t1 = ys[0] * d[1] + ys[1] * d[2] + ys[2] * d[3]
                t2 = ys[3] * d[4] + ys[4] * d[5] + ys[5] * d[6] + ys[6] * d[7] + ys[7] * d[8]
                if t == 1 and g == 0:
                    cot_feat[g, rows, p * atoms : (p + 1) * atoms] = (
                        r[0] * d[0] + r[1] * t1 + r[2] * t2
                    ).astype(BF16)
                total[0] = total[0] + v * (q[0] * d[0] + q[1] * t1 + q[2] * t2)
                p1, p2 = v * r[1], v * r[2]
                for m in range(1, 9):
                    total[m] = total[m] + (p1 if m < 4 else p2) * d[m]
            for m in range(9):
                whole = total[m][:8] + total[m][8:]
                spots = slice(p * 8, (p + 1) * 8)
                if adding:
                    whole = whole + acc_ref[g, m, spots]
                acc_ref[g, m, spots] = whole

    def early_cot():
        base = tiles(1, 1)
        for p in range(pairs):
            ys = [twin(harm[pairs + p, m * 8 : (m + 1) * 8]) for m in range(8)]
            for c in range(0, channels, 16):
                a = [amp[3, m, c : c + 16] for m in range(1, 9)]
                t1 = ys[0] * a[0] + ys[1] * a[1] + ys[2] * a[2]
                t2 = ys[3] * a[3] + ys[4] * a[4] + ys[5] * a[5] + ys[6] * a[6] + ys[7] * a[7]
                for l, t in ((1, t1), (2, t2)):
                    at_l = l * channels + c
                    at_s = at_l - channels
                    part[p, at_s : at_s + 16] = rad[base + p, at_l : at_l + 16] * t

    def late_cot(dinv):
        base = tiles(1, 1)
        for c in range(0, channels, 16):
            d0 = dinv[c : c + 16]
            d1 = 2.0 * dinv[channels + c : channels + c + 16]
            d2 = 2.0 * dinv[2 * channels + c : 2 * channels + c + 16]
            for p in range(pairs):
                cot_feat[1, c : c + 16, p * atoms : (p + 1) * atoms] = (
                    rad[base + p, c : c + 16] * d0
                    + part[p, c : c + 16] * d1
                    + part[p, channels + c : channels + c + 16] * d2
                ).astype(BF16)

    def slopes():
        base = tiles(0, 2)
        for p in range(counts[2]):
            ys = [twin(harm[2 * pairs + p, m * 8 : (m + 1) * 8]) for m in range(8)]
            for c in range(0, channels, 16):
                v = 2.0 * feat[base + p, c : c + 16]
                r = [rad[base + p, l * channels + c : l * channels + c + 16] for l in range(3)]
                q = [drad[base + p, l * channels + c : l * channels + c + 16] for l in range(3)]
                a = [amp[4, m, c : c + 16] for m in range(1, 9)]
                t1 = ys[0] * a[0] + ys[1] * a[1] + ys[2] * a[2]
                t2 = ys[3] * a[3] + ys[4] * a[4] + ys[5] * a[5] + ys[6] * a[6] + ys[7] * a[7]
                p1, p2 = ROOT3 * (v * r[1]), ROOT5 * (v * r[2])
                out = (
                    0.5 * v * q[0],
                    v * q[1] * t1,
                    v * q[2] * t2,
                    p1 * a[0],
                    p1 * a[1],
                    p1 * a[2],
                    p2 * (ys[1] * a[3] + ys[2] * a[6] + ys[0] * a[7]),
                    p2 * (ys[0] * a[3] + ys[2] * a[4] - ys[1] * a[7]),
                    p2 * (ys[1] * a[4] + ys[0] * a[6] + ROOT3 * (ys[2] * a[5])),
                )
                for i, x in enumerate(out):
                    edge_jac[p, i, c : c + 16] = x

    def edge_backward(dinv):
        for p in range(counts[2]):
            total = [jnp.zeros((16, atoms), F32) for _ in range(4)]
            for c in range(0, channels, 16):
                d = [dinv[l * channels + c : l * channels + c + 16] for l in range(3)]
                x = [edge_jac[p, i, c : c + 16] for i in range(9)]
                total[0] = total[0] + (x[0] * d[0] + x[1] * d[1] + x[2] * d[2])
                for k in range(3):
                    total[1 + k] = total[1 + k] + (x[3 + k] * d[1] + x[6 + k] * d[2])
            for m in range(4):
                acc_ref[2, m, p * 8 : (p + 1) * 8] = total[m][:8] + total[m][8:]

    def edge_grads(g):
        n = counts[g]
        d = []
        for m in range(4 if g == 2 else 9):
            d.append(sum(acc_ref[g, m, pl.ds(j, n, stride=8), :] for j in range(8)))
        nx, ny, nz, over = [v[:n] for v in geo[g]]
        if g == 2:
            gx, gy, gz = d[1:]
        else:
            gx = ROOT3 * d[1] + ROOT15 * (ny * d[4] + nz * d[7] + nx * d[8])
            gy = ROOT3 * d[2] + ROOT15 * (nx * d[4] + nz * d[5] - ny * d[8])
            gz = ROOT3 * d[3] + ROOT15 * (ny * d[5] + nx * d[7]) + (3.0 * ROOT5) * nz * d[6]
        along = d[0] - (nx * gx + ny * gy + nz * gz) * over
        grad = [a * along + b * over for a, b in ((nx, gx), (ny, gy), (nz, gz))]
        basis[g, 0, 0:64] = jnp.zeros((64, atoms), F32)
        for k in range(3):
            basis[g, 0, k * 8 : k * 8 + n] = -grad[k]
        for p in range(n):
            row = basis[g, 0, pl.ds(p, 8, stride=8), :]
            high = row.astype(BF16).astype(F32)
            both = jnp.concatenate([high, row - high], axis=0).astype(BF16)
            lanes = slice(p * atoms, (p + 1) * atoms)
            grad_cat[g, 0:16, lanes] = both
            grad_cat[g, 16:32, lanes] = both
        return [fold(jnp.sum(v, axis=0, keepdims=True), g) for v in grad]

    pl.semaphore_wait(barrier, len(slabs))
    send(0, False)
    onehot(2)
    radial(2, (0,))
    gather(0, 2, start_b)
    mix_t[...] = weight_rows(mixing[0]).T.astype(BF16)
    onehot(1)
    radial(1, (0, 1))
    gather(0, 1, start_b)
    onehot(0)
    radial(0, (0,))
    gather(0, 0, start_b)

    wait_in(0)
    ghost_t = arrived(0)
    gather(0, 2, ghost_t, True)
    first_edge = start_edge + dot(mix_t[...], split_rows(forward(0, 2)))
    fill(1, dot_nt(rep[0], first_edge.astype(BF16)))
    send(1, False)
    gather(0, 1, ghost_t, True)
    inv_own = forward(0, 0)
    inv_both = jnp.where(low_of(inv_own), inv_own, forward(0, 1))
    first_b = (start_t + dot(mix_t[...], split_rows(inv_both))).astype(BF16)
    first_ref[...] = first_b.astype(F32)
    gather(1, 1, first_b)

    rl_col = jnp.broadcast_to(read_linear[...], (channels, channels)).T
    rh = read_hidden[...]
    rh_high = rh.astype(BF16).astype(F32)
    rh_two = jnp.concatenate([rh_high, rh - rh_high], axis=1).astype(BF16)
    rh_t = jnp.concatenate([rh_high, rh_high, rh - rh_high], axis=1).astype(BF16)
    rh_c = weight_rows(rh).T.astype(BF16)
    ro_col = jnp.broadcast_to(read_out[...], (channels, read_out.shape[1])).T
    high = mixing[1].astype(BF16).astype(F32)
    mixed = dot_nt(
        rh_t, jnp.concatenate([high, mixing[1] - high, high], axis=1).astype(BF16)
    )
    high = mixed.astype(BF16).astype(F32)
    act_w = jnp.concatenate([high, high, mixed - high], axis=1).astype(BF16)
    dact_w = weight_rows(mixed).T.astype(BF16)

    def energy_own(g):
        own = dup(first_ref[...], g)
        doubled = jnp.concatenate([own, own], axis=0).astype(BF16)
        return jnp.sum(rl_col * own, axis=0, keepdims=True), dot(rh_two, doubled)

    def energy(features, site, act):
        act = act + dot(act_w, split_rows(features))
        gate = 0.5 + 0.5 * jnp.tanh(0.5 * act)
        value = act * gate
        site = site + jnp.sum(ro_col * value, axis=0, keepdims=True)
        dact = split_rows(ro_col * gate * (1.0 + act - value))
        return site, dact, dot(dact_w, dact)

    before = energy_own(1)
    wait_in(1)
    gather(1, 1, arrived(1), True)
    features = forward(1, 1)
    early_cot()
    site_ghost, dact_ghost, dinv_ghost = energy(features, *before)
    late_cot(dinv_ghost)
    fill(2, dot_nt(oh_ghost[atoms:], cot_feat[1]))
    send(2, True)

    slopes()
    high = mixing[0].astype(BF16).astype(F32)
    mix_c[...] = jnp.concatenate([high, high, mixing[0] - high], axis=1).astype(BF16)
    radial(0, (1,))
    gather(1, 0, first_b)
    site_own, dact_own, dinv = energy(forward(1, 0), *energy_own(0))
    backward(1, 0, dinv, False)
    backward(1, 1, dinv_ghost, False)
    cot_own, cot_ghost = dot(rh_c, dact_own), dot(rh_c, dact_ghost)
    cot = rl_col + jnp.where(low_of(cot_own), cot_own, cot_ghost)
    cot = cot + dot_nt(cot_feat[0], oh_own[...]) + dot_nt(cot_feat[1], oh_ghost[:atoms])

    def local_backward(g):
        backward(0, g, dot(mix_c[...], split_rows(dup(cot, g))), True)
        return edge_grads(g)

    sums_ghost = local_backward(1)
    outward = dot_nt(oh_ghost[atoms:], grad_cat[1])

    wait_in(2)
    edge_backward(dot(mix_c[...], split_rows(dot(arrived(2), rep[1]))))
    sums = edge_grads(2)
    width = counts[2] * atoms
    outward = outward + dot_nt(oh_edge[atoms:], grad_cat[2, :, :width])
    rest = outward - outward.astype(BF16).astype(F32)
    fill(3, jnp.where(lax.broadcasted_iota(jnp.int32, rest.shape, 1) < 16, outward, rest))
    send(3, True)

    site_out[...] = jnp.where(low_of(site_own), site_own, site_ghost)
    sums_own = local_backward(0)
    local = dot_nt(grad_cat[0, :16], oh_own[...]) + dot_nt(grad_cat[1, :16], oh_ghost[:atoms])
    local = local + dot_nt(grad_cat[2, :16, :width], oh_edge[:atoms])
    mine = jnp.concatenate(
        [jnp.where(low_of(sums_own[k]), sums_own[k], sums_ghost[k]) for k in range(3)], axis=0
    )
    local = local[:3] + local[8:11] + mine
    rows = jnp.concatenate(sums + [jnp.zeros((5, atoms), F32)], axis=0)
    rows = jnp.where(lane < few, rows, 0.0)
    high = rows.astype(BF16).astype(F32)
    mid = (rows - high).astype(BF16).astype(F32)
    parts = jnp.concatenate([high, mid, rows - high - mid], axis=0).astype(BF16)
    parts = dot(parts, sel_b[...])
    local = local + (parts[:3] + parts[8:11] + parts[16:19])
    for phase in range(4):
        wait_out(phase)
    wait_in(3)
    back = dot(arrived(3)[:32], sel[...])
    back = back[:16] + back[16:]
    force_out[...] = local + (back[:3] + back[8:11])


def finish(site_in, force_in, site_out, force_out):
    site_out[...] = site_in[0]
    force_out[...] = force_in[...]


def solution(mesh):
    sizes = tuple(mesh.shape[axis] for axis in AXES)

    def body(
        species,
        send_list,
        neighbours,
        edge_vectors,
        embedding,
        radial_in,
        radial_mid,
        radial_out,
        mixing,
        read_linear,
        read_hidden,
        read_out,
    ):
        atoms = species.shape[0]
        channels = embedding.shape[1]
        slots = neighbours.shape[0]
        pairs = slots // 2
        hidden = radial_mid.shape[1]
        cell_rows = send_list.shape[3]
        ghosts = plan_slabs(cell_rows)[1]
        kinds = ((6, 4 * cell_rows), (12, 2 * cell_rows), (8, 2 * cell_rows))
        vmem = pl.BlockSpec(memory_space=pltpu.VMEM)
        operands = (
            species.reshape(1, atoms),
            send_list,
            neighbours,
            edge_vectors,
            embedding,
            radial_in,
            radial_mid,
            radial_out,
            mixing,
            read_linear.reshape(1, channels),
            read_hidden.T,
            read_out.reshape(1, read_out.shape[0]),
        )
        site, forces = pl.pallas_call(
            functools.partial(kernel, sizes),
            out_shape=(pltpu.VMEM((1, atoms), F32), pltpu.VMEM((3, atoms), F32)),
            in_specs=[tuple(pl.BlockSpec(memory_space=pltpu.HBM) for _ in operands)],
            out_specs=(vmem, vmem),
            scratch_shapes=[
                pltpu.VMEM((3, 2, 8 * pairs, atoms), F32),
                pltpu.VMEM((3, 2, pairs, atoms), F32),
                pltpu.VMEM((3 * pairs, 64, atoms), F32),
                pltpu.VMEM((5 * pairs, 3 * channels, atoms), F32),
                pltpu.VMEM((5 * pairs, 3 * channels, atoms), F32),
                pltpu.VMEM((atoms, pairs * atoms), BF16),
                pltpu.VMEM((atoms + ghosts, pairs * atoms), BF16),
                pltpu.VMEM((atoms + ghosts, pairs * atoms // 2), BF16),
                pltpu.VMEM((5 * pairs, channels, atoms), F32),
                pltpu.VMEM((5, 9, channels, atoms), F32),
                pltpu.VMEM((2, channels, pairs * atoms), BF16),
                pltpu.VMEM((3, 9, 8 * pairs, atoms), F32),
                pltpu.VMEM((3, 32, pairs * atoms), BF16),
                pltpu.VMEM((ghosts, atoms), BF16),
                pltpu.VMEM((atoms, atoms), BF16),
                pltpu.VMEM((2, ghosts, atoms), BF16),
                pltpu.VMEM((2 * hidden, 32), BF16),
                pltpu.VMEM((2, hidden, 3 * hidden), BF16),
                pltpu.VMEM((2, 3 * channels, 3 * hidden), BF16),
                pltpu.VMEM((channels, 9 * channels), BF16),
                pltpu.VMEM((3 * channels, 3 * channels), BF16),
                pltpu.VMEM((channels, atoms), F32),
                tuple(pltpu.VMEM((4, n, depth, channels), BF16) for n, depth in kinds),
                tuple(pltpu.VMEM((4, n, depth, channels), BF16) for n, depth in kinds),
                pltpu.SemaphoreType.DMA((4, len(kinds))),
                pltpu.SemaphoreType.DMA((4, len(kinds))),
                pltpu.VMEM((pairs, 2 * channels, atoms), F32),
                pltpu.VMEM((pairs // 2, 9, channels, atoms), F32),
                tuple(
                    (pltpu.SMEM if x is send_list else pltpu.VMEM)(x.shape, x.dtype)
                    for x in operands
                ),
                pltpu.SemaphoreType.DMA((len(operands),)),
            ],
            compiler_params=pltpu.CompilerParams(
                collective_id=0, has_side_effects=True, vmem_limit_bytes=56 * 1024 * 1024
            ),
        )(operands)
        site, forces = [pltpu.with_memory_space_constraint(x, pltpu.VMEM) for x in (site, forces)]
        return pl.pallas_call(
            finish,
            out_shape=(
                jax.ShapeDtypeStruct((atoms,), F32),
                jax.ShapeDtypeStruct((3, atoms), F32),
            ),
            in_specs=[vmem, vmem],
            out_specs=(vmem, vmem),
        )(site, forces)

    in_specs = (
        P(AXES),
        P("gx", "gy", "gz", None),
        P(None, AXES),
        P(None, None, AXES),
        P(),
        P(),
        P(),
        P(),
        P(),
        P(),
        P(),
        P(),
    )
    out_specs = (P(AXES), P(None, AXES))
    return jax.shard_map(body, mesh=mesh, in_specs=in_specs, out_specs=out_specs, check_vma=False)
```

```python
import functools
import itertools

import jax
import jax.numpy as jnp
from jax import lax
from jax.experimental import pallas as pl
from jax.experimental.pallas import tpu as pltpu
from jax.sharding import PartitionSpec as P

CUTOFF = 5.0
AXES = ("gx", "gy", "gz")
F32 = jnp.float32
BF16 = jnp.bfloat16
MESH = pl.DeviceIdType.MESH
ROOT3 = 3.0**0.5
ROOT5 = 5.0**0.5
ROOT15 = 15.0**0.5
PI = 3.141592653589793
WIDE = 8
LOAD_ORDER = (1, 0, 4, 2, 3, 5, 6, 7, 9, 8, 10, 11)


def plan_slabs(cell_rows):
    picks = {1: (1,), -1: (0,), 0: (0, 1)}
    slabs, offset = [], 0
    for count in (1, 2, 3):
        for step in itertools.product((-1, 0, 1), repeat=3):
            if sum(s != 0 for s in step) != count:
                continue
            cells = list(itertools.product(*[picks[s] for s in step]))
            if len(cells) == 1:
                cells.append(None)
            blocks = [tuple(cells[i : i + 2]) for i in range(0, len(cells), 2)]
            slabs.append((step, offset, 8 * len(blocks), blocks))
            offset += 8 * len(blocks)
    return slabs, offset


def ghost_row(step, cell, atoms, cell_rows):
    spots = [{1: 0, -1: 3, 0: c + 1}[s] for s, c in zip(step, cell)]
    return atoms + (16 * spots[0] + 4 * spots[1] + spots[2]) * cell_rows


def split_rows(x):
    high = x.astype(BF16).astype(F32)
    return jnp.concatenate([high, x - high, high], axis=0).astype(BF16)


def weight_rows(w):
    high = w.astype(BF16).astype(F32)
    return jnp.concatenate([high, high, w - high], axis=0)


def dot(a, b):
    return lax.dot_general(a, b, (((1,), (0,)), ((), ())), preferred_element_type=F32)


def dot_nt(a, b):
    return lax.dot_general(a, b, (((1,), (1,)), ((), ())), preferred_element_type=F32)


def mult(x, n):
    return x if isinstance(x, int) else pl.multiple_of(x, n)


def loop(count, body):
    for i in range(count):
        body(i)


def kernel(
    sizes,
    operands,
    site_out,
    force_out,
    basis,
    cut,
    harm,
    rad,
    drad,
    oh_own,
    oh_ghost,
    oh_edge,
    feat,
    amp,
    cot_feat,
    acc_ref,
    grad_cat,
    sel,
    sel_b,
    rep,
    rep_t,
    w_in,
    w_mid,
    w_out,
    mix_t,
    mix_c,
    first_ref,
    send_buf,
    recv_buf,
    send_sem,
    recv_sem,
    part,
    edge_jac,
    held,
    held_sem,
):
    (
        species,
        send_list,
        neighbours,
        vectors,
        embedding,
        radial_in,
        radial_mid,
        radial_out,
        mixing,
        read_linear,
        read_hidden,
        read_out,
    ) = held
    atoms = species.shape[1]
    half = atoms // 2
    channels = embedding.shape[1]
    pairs = neighbours.shape[0] // 2
    cell_rows = send_list.shape[3]
    hidden = radial_mid.shape[1]
    slabs, ghosts = plan_slabs(cell_rows)
    ways = []
    for step, _, _, _ in slabs:
        kind = sum(s != 0 for s in step) - 1
        ways.append((kind, sum(way[0] == kind for way in ways), step))
    me = [lax.axis_index(axis) for axis in AXES]

    def at(step):
        return tuple(
            m if s == 0 else lax.rem(m + (s + n), n) for m, s, n in zip(me, step, sizes)
        )

    barrier = pltpu.get_barrier_semaphore()
    for step, _, _, _ in slabs:
        pl.semaphore_signal(barrier, inc=1, device_id=at(step), device_id_type=MESH)

    loads = [
        pltpu.make_async_copy(source, goal, held_sem.at[i])
        for i, (source, goal) in enumerate(zip(operands, held))
    ]
    for i in LOAD_ORDER:
        loads[i].start()

    def send(phase, back):
        for kind, index, step in ways:
            goal = tuple(-s for s in step) if back else step
            pltpu.make_async_remote_copy(
                src_ref=send_buf[kind].at[phase, index],
                dst_ref=recv_buf[kind].at[phase, index],
                send_sem=send_sem.at[phase, kind],
                recv_sem=recv_sem.at[phase, kind],
                device_id=at(goal),
                device_id_type=MESH,
            ).start()

    def wait_all(bufs, sems, phase):
        for kind, buf in enumerate(bufs):
            whole = buf.at[phase]
            pltpu.make_async_copy(whole, whole, sems.at[phase, kind]).wait()

    def wait_in(phase):
        wait_all(recv_buf, recv_sem, phase)

    def wait_out(phase):
        wait_all(send_buf, send_sem, phase)

    def fill(phase, rows):
        start = 0
        for buf in send_buf:
            count, depth = buf.shape[1:3]
            part_rows = rows[start : start + count * depth]
            buf[phase, :, :, : rows.shape[1]] = part_rows.reshape(
                count, depth, rows.shape[1]
            ).astype(BF16)
            start += count * depth

    def arrived(phase, turned=True):
        parts = []
        for buf in recv_buf:
            block = buf[phase]
            count, depth, width = block.shape
            if depth % 16:
                block = block.astype(F32).reshape(count * depth, width).astype(BF16)
            parts.append(block.reshape(count * depth, width))
        whole = jnp.concatenate(parts, axis=0)
        return whole.T if turned else whole

    lane = lax.broadcasted_iota(jnp.int32, (8, atoms), 1)
    sub = lax.broadcasted_iota(jnp.int32, (8, atoms), 0)
    low8 = lane < half
    few = 8 * cell_rows
    turns = (half, half, few)
    counts = (pairs, pairs, 2 * neighbours.shape[0] * few // (2 * atoms))
    spread = 4 * pairs

    def low_of(x):
        return lax.broadcasted_iota(jnp.int32, x.shape, 1) < half

    def turn(x):
        return pltpu.roll(x, half, 1)

    def fold(x, group):
        x = x + turn(x)
        return x + pltpu.roll(x, few, 1) if group == 2 else x

    def dup(x, group):
        if group == 0:
            return jnp.where(low_of(x), x, turn(x))
        return jnp.where(low_of(x), turn(x), x)

    def paired(x):
        top, bottom = x[:pairs], x[pairs:]
        return (
            jnp.where(low8, top, turn(bottom)),
            jnp.where(low8, turn(top), bottom),
        )

    for i in LOAD_ORDER:
        loads[i].wait()

    cell_ids = {}
    spot = sub % cell_rows
    cells = list(itertools.product((0, 1), repeat=3))
    for cell in cells:
        value = jnp.full((8, atoms), send_list[cell + (0,)], jnp.int32)
        for k in range(1, cell_rows):
            value = jnp.where(spot == k, send_list[cell + (k,)], value)
        cell_ids[cell] = value
    none = jnp.full((8, atoms), -1, jnp.int32)
    cell_ids[None] = none

    def place(cell, shift):
        return none if cell is None else cells.index(cell) * cell_rows + sub - shift

    row_ids, chosen, rep_one, rep_all = [], [], [], []
    within = lane % few
    for step, offset, rows, blocks in slabs:
        for cell_a, cell_b in blocks:
            ids = jnp.where(sub < cell_rows, cell_ids[cell_a], cell_ids[cell_b])
            chosen.append(jnp.where(ids == lane, 1.0, 0.0))
            spots = jnp.where(sub < cell_rows, place(cell_a, 0), place(cell_b, cell_rows))
            rep_one.append(jnp.where(spots == lane, 1.0, 0.0))
            rep_all.append(jnp.where(spots == within, 1.0, 0.0))
            base_a = ghost_row(step, cell_a, atoms, cell_rows) + sub
            if cell_b is None:
                base_b = none
            else:
                base_b = ghost_row(step, cell_b, atoms, cell_rows) + sub - cell_rows
            row_ids.append(jnp.where(sub < cell_rows, base_a, base_b))
    sel[...] = jnp.concatenate(chosen, axis=0).astype(BF16)
    rep[...] = jnp.concatenate(rep_one, axis=0).astype(BF16)
    rep_t[...] = jnp.concatenate(rep_all, axis=0).T.astype(BF16)
    boundary = []
    for i in range(0, 8, 2):
        ids = jnp.where(sub < cell_rows, cell_ids[cells[i]], cell_ids[cells[i + 1]])
        boundary.append(jnp.where(ids == lane, 1.0, 0.0))
    sel_b[...] = jnp.concatenate(boundary * (atoms // few), axis=0).astype(BF16)

    kinds = jnp.where(sub == jnp.broadcast_to(species[...], (8, atoms)), 1.0, 0.0).astype(BF16)
    emb_t = embedding[...].astype(F32).T.astype(BF16)
    start_t = dot(emb_t, kinds)
    start_b = start_t.astype(BF16)
    start_edge = dot_nt(start_b, sel_b[...])
    fill(0, dot_nt(rep[...], start_edge.astype(BF16)))

    for t in range(2):
        pad = jnp.zeros((8, hidden), F32)
        w_in[t * hidden : (t + 1) * hidden] = (
            jnp.concatenate([weight_rows(radial_in[t]), pad], axis=0).T.astype(BF16)
        )
        w_mid[t] = weight_rows(radial_mid[t]).T.astype(BF16)
        w_out[t] = weight_rows(radial_out[t]).T.astype(BF16)

    nbr_f = neighbours[...].astype(F32)
    raw = jnp.concatenate([vectors[0], vectors[1], vectors[2], nbr_f], axis=0)
    raw_high = raw.astype(BF16).astype(F32)
    raw_mid = (raw - raw_high).astype(BF16).astype(F32)
    pieces = jnp.concatenate([raw_high, raw_mid, raw - raw_high - raw_mid], axis=0)
    pieces = dot_nt(pieces.astype(BF16), sel_b[...])
    depth = raw.shape[0]
    edge_raw = pieces[:depth] + pieces[depth : 2 * depth] + pieces[2 * depth :]

    def quarters(x):
        rows = counts[2]
        out = x[:rows]
        for i in range(1, atoms // few):
            out = jnp.where(lane[:rows] // few == i, x[i * rows : (i + 1) * rows], out)
        return jnp.concatenate([out, out], axis=0)

    slots = neighbours.shape[0]
    edge_parts = [quarters(edge_raw[k * slots : (k + 1) * slots]) for k in range(4)]
    vec = [paired(vectors[k]) + (edge_parts[k],) for k in range(3)]
    nbr = paired(nbr_f) + (edge_parts[3],)
    geo = []
    for g in range(3):
        x, y, z = vec[0][g], vec[1][g], vec[2][g]
        length = jnp.sqrt(x * x + y * y + z * z)
        over = 1.0 / length
        nx, ny, nz = x * over, y * over, z * over
        geo.append((nx, ny, nz, over))
        u = length * (1.0 / CUTOFF)
        u2 = u * u
        u4 = u2 * u2
        u5 = u4 * u
        inside = u < 1.0
        env = 1.0 - 21.0 * u5 + 35.0 * u5 * u - 15.0 * u5 * u2
        denv = (-105.0 / CUTOFF) * u4 * (1.0 - u) * (1.0 - u)
        cut[g, 0] = jnp.where(inside, 0.25 * env, 0.0)
        cut[g, 1] = jnp.where(inside, 0.25 * denv, 0.0)
        theta = PI * u
        sin1, cos1 = jnp.sin(theta), jnp.cos(theta)
        twice = 2.0 * cos1
        s_old, s_now = jnp.zeros_like(sin1), sin1
        c_old, c_now = jnp.ones_like(cos1), cos1
        amp0 = (2.0 / CUTOFF) ** 0.5
        for k in range(1, 9):
            base = amp0 * s_now * over
            slope = (amp0 * k * PI / CUTOFF * c_now - base) * over
            basis[g, 0, (k - 1) * 8 : k * 8] = base
            basis[g, 1, (k - 1) * 8 : k * 8] = slope
            s_old, s_now = s_now, twice * s_now - s_old
            c_old, c_now = c_now, twice * c_now - c_old
        ylm = (
            ROOT3 * nx,
            ROOT3 * ny,
            ROOT3 * nz,
            ROOT15 * nx * ny,
            ROOT15 * ny * nz,
            0.5 * ROOT5 * (3.0 * nz * nz - 1.0),
            ROOT15 * nx * nz,
            0.5 * ROOT15 * (nx * nx - ny * ny),
        )
        for m in range(8):
            for p in range(counts[g]):
                harm[g * pairs + p, m * 8 : (m + 1) * 8] = jnp.broadcast_to(
                    ylm[m][p : p + 1], (8, atoms)
                )

    own_rows = jnp.concatenate([sub + 8 * b for b in range(atoms // 8)], axis=0).astype(F32)
    all_rows = jnp.concatenate([own_rows] + [r.astype(F32) for r in row_ids], axis=0)
    onehots = (oh_own, oh_ghost, oh_edge)

    def onehot(g):
        ids = own_rows if g == 0 else all_rows
        for p in range(counts[g]):
            onehots[g][:, p * atoms : (p + 1) * atoms] = jnp.where(
                ids == nbr[g][p : p + 1], 1.0, 0.0
            ).astype(BF16)

    def silu_pair(x, dx):
        gate = 0.5 + 0.5 * jnp.tanh(0.5 * x)
        value = x * gate
        return value, gate * (1.0 + x - value) * dx

    def tiles(t, g):
        return spread if g == 2 else (t * 2 + g) * pairs

    def radial(g, layers):
        top = layers[-1] * hidden + hidden

        def chunk(j):
            spots = range(j * WIDE, min(counts[g], (j + 1) * WIDE))

            def wide(kind):
                return jnp.concatenate(
                    [basis[g, kind, pl.ds(p, 8, stride=8), :] for p in spots], axis=1
                )

            def row(kind):
                return jnp.concatenate([cut[g, kind, p : p + 1, :] for p in spots], axis=1)

            env, denv = row(0), row(1)

            def first_dot(x):
                high = x.astype(BF16).astype(F32)
                full = jnp.concatenate([high, x - high, high, jnp.zeros_like(x)], axis=0)
                return dot(w_in[:top], full.astype(BF16))

            one, done = silu_pair(first_dot(wide(0)), first_dot(wide(1)))
            for t in layers:
                rows = slice(t * hidden, (t + 1) * hidden)
                two, dtwo = silu_pair(
                    dot(w_mid[t], split_rows(one[rows])), dot(w_mid[t], split_rows(done[rows]))
                )
                value = dot(w_out[t], split_rows(env * two))
                slope = dot(w_out[t], split_rows(denv * two + env * dtwo))
                for i, p in enumerate(spots):
                    lanes = slice(i * atoms, (i + 1) * atoms)
                    rad[tiles(t, g) + p] = value[:, lanes]
                    drad[tiles(t, g) + p] = slope[:, lanes]

        loop(-(-counts[g] // WIDE), chunk)

    def gather(t, g, rows_t, ghosts_too=False):
        base = tiles(t, g)
        if ghosts_too:
            out = dot(rows_t, onehots[g][atoms:])
        else:
            out = dot(rows_t, onehots[g][:atoms])
        for p in range(counts[g]):
            tile = out[:, p * atoms : (p + 1) * atoms]
            feat[base + p] = feat[base + p] + tile if ghosts_too else tile

    def twin(y):
        return jnp.concatenate([y, y], axis=0)

    def forward(t, g):
        which = 4 if g == 2 else t * 2 + g
        base = tiles(t, g)
        parts_out = ([], [], [])
        for c in range(0, channels, 16):
            total = [jnp.zeros((16, atoms), F32) for _ in range(9)]
            for p in range(counts[g]):
                v = feat[base + p, c : c + 16]
                parts = [
                    rad[base + p, l * channels + c : l * channels + c + 16] * v for l in range(3)
                ]
                total[0] = total[0] + parts[0]
                for m in range(8):
                    y = twin(harm[g * pairs + p, m * 8 : (m + 1) * 8])
                    total[1 + m] = total[1 + m] + y * parts[1 if m < 3 else 2]
            total = [fold(a, g) for a in total]
            for m in range(1, 9):
                amp[which, m, c : c + 16] = total[m]
            parts_out[0].append(total[0])
            parts_out[1].append(sum(a * a for a in total[1:4]))
            parts_out[2].append(sum(a * a for a in total[4:9]))
        return jnp.concatenate(parts_out[0] + parts_out[1] + parts_out[2], axis=0)

    def backward(t, g, dinv, adding):
        which = 4 if g == 2 else t * 2 + g
        base = tiles(t, g)
        for c in range(0, channels, 16):
            rows = slice(c, c + 16)
            amp[which, 0, rows] = dinv[rows]
            d1 = 2.0 * dinv[channels + c : channels + c + 16]
            d2 = 2.0 * dinv[2 * channels + c : 2 * channels + c + 16]
            for m in range(1, 9):
                amp[which, m, rows] = amp[which, m, rows] * (d1 if m < 4 else d2)
        for p in range(counts[g]):
            ys = [twin(harm[g * pairs + p, m * 8 : (m + 1) * 8]) for m in range(8)]
            total = [jnp.zeros((16, atoms), F32) for _ in range(9)]
            for c in range(0, channels, 16):
                rows = slice(c, c + 16)
                v = feat[base + p, rows]
                r = [rad[base + p, l * channels + c : l * channels + c + 16] for l in range(3)]
                q = [drad[base + p, l * channels + c : l * channels + c + 16] for l in range(3)]
                d = [amp[which, m, rows] for m in range(9)]
                t1 = ys[0] * d[1] + ys[1] * d[2] + ys[2] * d[3]
                t2 = ys[3] * d[4] + ys[4] * d[5] + ys[5] * d[6] + ys[6] * d[7] + ys[7] * d[8]
                if t == 1 and g == 0:
                    cot_feat[g, rows, p * atoms : (p + 1) * atoms] = (
                        r[0] * d[0] + r[1] * t1 + r[2] * t2
                    ).astype(BF16)
                total[0] = total[0] + v * (q[0] * d[0] + q[1] * t1 + q[2] * t2)
                p1, p2 = v * r[1], v * r[2]
                for m in range(1, 9):
                    total[m] = total[m] + (p1 if m < 4 else p2) * d[m]
            for m in range(9):
                whole = total[m][:8] + total[m][8:]
                spots = slice(p * 8, (p + 1) * 8)
                if adding:
                    whole = whole + acc_ref[g, m, spots]
                acc_ref[g, m, spots] = whole

    def early_cot():
        base = tiles(1, 1)
        for p in range(pairs):
            ys = [twin(harm[pairs + p, m * 8 : (m + 1) * 8]) for m in range(8)]
            for c in range(0, channels, 16):
                a = [amp[3, m, c : c + 16] for m in range(1, 9)]
                t1 = ys[0] * a[0] + ys[1] * a[1] + ys[2] * a[2]
                t2 = ys[3] * a[3] + ys[4] * a[4] + ys[5] * a[5] + ys[6] * a[6] + ys[7] * a[7]
                for l, t in ((1, t1), (2, t2)):
                    at_l = l * channels + c
                    at_s = at_l - channels
                    part[p, at_s : at_s + 16] = rad[base + p, at_l : at_l + 16] * t

    def late_cot(dinv):
        base = tiles(1, 1)
        for c in range(0, channels, 16):
            d0 = dinv[c : c + 16]
            d1 = 2.0 * dinv[channels + c : channels + c + 16]
            d2 = 2.0 * dinv[2 * channels + c : 2 * channels + c + 16]
            for p in range(pairs):
                cot_feat[1, c : c + 16, p * atoms : (p + 1) * atoms] = (
                    rad[base + p, c : c + 16] * d0
                    + part[p, c : c + 16] * d1
                    + part[p, channels + c : channels + c + 16] * d2
                ).astype(BF16)

    def slopes():
        base = tiles(0, 2)
        for p in range(counts[2]):
            ys = [twin(harm[2 * pairs + p, m * 8 : (m + 1) * 8]) for m in range(8)]
            unit = [y * (1.0 / ROOT3) for y in ys[:3]]
            over = jnp.broadcast_to(geo[2][3][p : p + 1], (16, atoms))
            for c in range(0, channels, 16):
                v = 2.0 * feat[base + p, c : c + 16]
                r = [rad[base + p, l * channels + c : l * channels + c + 16] for l in range(3)]
                q = [drad[base + p, l * channels + c : l * channels + c + 16] for l in range(3)]
                a = [amp[4, m, c : c + 16] for m in range(1, 9)]
                t1 = ys[0] * a[0] + ys[1] * a[1] + ys[2] * a[2]
                t2 = ys[3] * a[3] + ys[4] * a[4] + ys[5] * a[5] + ys[6] * a[6] + ys[7] * a[7]
                p1, p2 = ROOT3 * (v * r[1]), ROOT5 * (v * r[2])
                along = (0.5 * v * q[0], v * q[1] * t1, v * q[2] * t2)
                across = (
                    None,
                    (p1 * a[0], p1 * a[1], p1 * a[2]),
                    (
                        p2 * (ys[1] * a[3] + ys[2] * a[6] + ys[0] * a[7]),
                        p2 * (ys[0] * a[3] + ys[2] * a[4] - ys[1] * a[7]),
                        p2 * (ys[1] * a[4] + ys[0] * a[6] + ROOT3 * (ys[2] * a[5])),
                    ),
                )
                for l in range(3):
                    rise, tilt = along[l], across[l]
                    if tilt is not None:
                        inward = unit[0] * tilt[0] + unit[1] * tilt[1] + unit[2] * tilt[2]
                        rise = rise - inward * over
                    for k in range(3):
                        x = unit[k] * rise
                        if tilt is not None:
                            x = x + tilt[k] * over
                        edge_jac[p, 3 * l + k, c : c + 16] = x

    def place_rows(g, p, rows):
        rows = jnp.concatenate(rows + [jnp.zeros((8, atoms), F32)], axis=0)
        high = rows.astype(BF16).astype(F32)
        both = jnp.concatenate([high, rows - high], axis=0).astype(BF16)
        lanes = slice(p * atoms, (p + 1) * atoms)
        grad_cat[g, :half, lanes] = both
        grad_cat[g, half:, lanes] = both

    def edge_backward(dinv):
        sums = [0.0, 0.0, 0.0]
        for p in range(counts[2]):
            total = [jnp.zeros((16, atoms), F32) for _ in range(3)]
            for c in range(0, channels, 16):
                d = [dinv[l * channels + c : l * channels + c + 16] for l in range(3)]
                for k in range(3):
                    x = [edge_jac[p, 3 * l + k, c : c + 16] for l in range(3)]
                    total[k] = total[k] + (x[0] * d[0] + x[1] * d[1] + x[2] * d[2])
            rows = [t[:8] + t[8:] for t in total]
            place_rows(2, p, [-r for r in rows])
            sums = [a + b for a, b in zip(sums, rows)]
        return sums

    def edge_grads(g):
        d = []
        for m in range(9):
            d.append(sum(acc_ref[g, m, pl.ds(j, pairs, stride=8), :] for j in range(8)))
        nx, ny, nz, over = geo[g]
        gx = ROOT3 * d[1] + ROOT15 * (ny * d[4] + nz * d[7] + nx * d[8])
        gy = ROOT3 * d[2] + ROOT15 * (nx * d[4] + nz * d[5] - ny * d[8])
        gz = ROOT3 * d[3] + ROOT15 * (ny * d[5] + nx * d[7]) + (3.0 * ROOT5) * nz * d[6]
        along = d[0] - (nx * gx + ny * gy + nz * gz) * over
        grad = [a * along + b * over for a, b in ((nx, gx), (ny, gy), (nz, gz))]
        for p in range(pairs):
            rows = [jnp.where(sub == 0, jnp.broadcast_to(-v[p : p + 1], (8, atoms)), 0.0) for v in grad]
            place_rows(g, p, rows)
        return [fold(jnp.sum(v, axis=0, keepdims=True), g) for v in grad]

    def components(x):
        x = x[: half // 2] + x[half // 2 : half]
        return jnp.concatenate(
            [jnp.sum(x[8 * k : 8 * k + 8], axis=0, keepdims=True) for k in range(3)], axis=0
        )

    onehot(2)
    radial(2, (0,))
    gather(0, 2, start_b)
    pl.semaphore_wait(barrier, len(slabs))
    send(0, False)
    mix_t[...] = weight_rows(mixing[0]).T.astype(BF16)
    onehot(1)
    radial(1, (0,))
    gather(0, 1, start_b)
    onehot(0)
    radial(0, (0,))
    gather(0, 0, start_b)

    wait_in(0)
    ghost_t = arrived(0)
    gather(0, 2, ghost_t, True)
    first_edge = start_edge + dot(mix_t[...], split_rows(forward(0, 2)))
    fill(1, dot_nt(rep[...], first_edge.astype(BF16)))
    send(1, False)
    gather(0, 1, ghost_t, True)
    inv_own = forward(0, 0)
    inv_both = jnp.where(low_of(inv_own), inv_own, forward(0, 1))
    first_b = (start_t + dot(mix_t[...], split_rows(inv_both))).astype(BF16)
    first_ref[...] = first_b.astype(F32)
    gather(1, 1, first_b)
    radial(1, (1,))

    rl_col = jnp.broadcast_to(read_linear[...], (channels, channels)).T
    rh = read_hidden[...]
    rh_high = rh.astype(BF16).astype(F32)
    rh_two = jnp.concatenate([rh_high, rh - rh_high], axis=1).astype(BF16)
    rh_t = jnp.concatenate([rh_high, rh_high, rh - rh_high], axis=1).astype(BF16)
    rh_c = weight_rows(rh).T.astype(BF16)
    ro_col = jnp.broadcast_to(read_out[...], (channels, read_out.shape[1])).T
    high = mixing[1].astype(BF16).astype(F32)
    mixed = dot_nt(
        rh_t, jnp.concatenate([high, mixing[1] - high, high], axis=1).astype(BF16)
    )
    high = mixed.astype(BF16).astype(F32)
    act_w = jnp.concatenate([high, high, mixed - high], axis=1).astype(BF16)
    dact_w = weight_rows(mixed).T.astype(BF16)

    def energy_own(g):
        own = dup(first_ref[...], g)
        doubled = jnp.concatenate([own, own], axis=0).astype(BF16)
        return jnp.sum(rl_col * own, axis=0, keepdims=True), dot(rh_two, doubled)

    def energy(features, site, act):
        act = act + dot(act_w, split_rows(features))
        gate = 0.5 + 0.5 * jnp.tanh(0.5 * act)
        value = act * gate
        site = site + jnp.sum(ro_col * value, axis=0, keepdims=True)
        dact = split_rows(ro_col * gate * (1.0 + act - value))
        return site, dact, dot(dact_w, dact)

    before = energy_own(1)
    wait_in(1)
    gather(1, 1, arrived(1), True)
    features = forward(1, 1)
    site_ghost, dact_ghost, dinv_ghost = energy(features, *before)
    early_cot()
    late_cot(dinv_ghost)
    fill(2, dot_nt(oh_ghost[atoms:], cot_feat[1]))
    send(2, True)

    slopes()
    high = mixing[0].astype(BF16).astype(F32)
    mix_c[...] = jnp.concatenate([high, high, mixing[0] - high], axis=1).astype(BF16)
    radial(0, (1,))
    gather(1, 0, first_b)
    site_own, dact_own, dinv = energy(forward(1, 0), *energy_own(0))
    backward(1, 0, dinv, False)
    backward(1, 1, dinv_ghost, False)
    cot_own, cot_ghost = dot(rh_c, dact_own), dot(rh_c, dact_ghost)
    cot = rl_col + jnp.where(low_of(cot_own), cot_own, cot_ghost)
    cot = cot + dot_nt(cot_feat[0], oh_own[...]) + dot_nt(cot_feat[1], oh_ghost[:atoms])

    def local_backward(g):
        backward(0, g, dot(mix_c[...], split_rows(dup(cot, g))), True)
        return edge_grads(g)

    sums_ghost = local_backward(1)
    outward = dot_nt(oh_ghost[atoms:], grad_cat[1])

    wait_in(2)
    back = dot(rep_t[...], arrived(2, False))
    high = back.astype(BF16).astype(F32)
    back = jnp.concatenate([high, back - high, high], axis=1).astype(BF16)
    sums = edge_backward(dot_nt(mix_c[...], back))
    width = counts[2] * atoms
    outward = outward + dot_nt(oh_edge[atoms:], grad_cat[2, :, :width])
    rest = outward - outward.astype(BF16).astype(F32)
    fill(3, jnp.where(low_of(rest), outward, rest))
    send(3, True)

    site_out[...] = jnp.where(low_of(site_own), site_own, site_ghost)
    sums_own = local_backward(0)
    local = dot_nt(grad_cat[0, :half], oh_own[...]) + dot_nt(grad_cat[1, :half], oh_ghost[:atoms])
    local = local + dot_nt(grad_cat[2, :half, :width], oh_edge[:atoms])
    mine = jnp.concatenate(
        [jnp.where(low_of(sums_own[k]), sums_own[k], sums_ghost[k]) for k in range(3)], axis=0
    )
    local = components(local) + mine
    sums = [fold(jnp.sum(v, axis=0, keepdims=True), 2) for v in sums]
    rows = jnp.concatenate(sums + [jnp.zeros((5, atoms), F32)], axis=0)
    rows = jnp.where(lane < few, rows, 0.0)
    high = rows.astype(BF16).astype(F32)
    mid = (rows - high).astype(BF16).astype(F32)
    parts = jnp.concatenate([high, mid, rows - high - mid], axis=0).astype(BF16)
    parts = dot(parts, sel_b[...])
    local = local + (parts[:3] + parts[8:11] + parts[16:19])
    for phase in range(4):
        wait_out(phase)
    wait_in(3)
    back = dot(arrived(3), sel[...])
    force_out[...] = local + components(back[:half] + back[half:])


def finish(site_in, force_in, site_out, force_out):
    site_out[...] = site_in[0]
    force_out[...] = force_in[...]


def solution(mesh):
    sizes = tuple(mesh.shape[axis] for axis in AXES)

    def body(
        species,
        send_list,
        neighbours,
        edge_vectors,
        embedding,
        radial_in,
        radial_mid,
        radial_out,
        mixing,
        read_linear,
        read_hidden,
        read_out,
    ):
        atoms = species.shape[0]
        channels = embedding.shape[1]
        slots = neighbours.shape[0]
        pairs = slots // 2
        hidden = radial_mid.shape[1]
        cell_rows = send_list.shape[3]
        ghosts = plan_slabs(cell_rows)[1]
        kinds = ((6, 4 * cell_rows), (12, 2 * cell_rows), (8, 2 * cell_rows))
        vmem = pl.BlockSpec(memory_space=pltpu.VMEM)
        operands = (
            species.reshape(1, atoms),
            send_list,
            neighbours,
            edge_vectors,
            embedding,
            radial_in,
            radial_mid,
            radial_out,
            mixing,
            read_linear.reshape(1, channels),
            read_hidden.T,
            read_out.reshape(1, read_out.shape[0]),
        )
        site, forces = pl.pallas_call(
            functools.partial(kernel, sizes),
            out_shape=(pltpu.VMEM((1, atoms), F32), pltpu.VMEM((3, atoms), F32)),
            in_specs=[tuple(pl.BlockSpec(memory_space=pltpu.HBM) for _ in operands)],
            out_specs=(vmem, vmem),
            scratch_shapes=[
                pltpu.VMEM((3, 2, 8 * pairs, atoms), F32),
                pltpu.VMEM((3, 2, pairs, atoms), F32),
                pltpu.VMEM((3 * pairs, 64, atoms), F32),
                pltpu.VMEM((5 * pairs, 3 * channels, atoms), F32),
                pltpu.VMEM((5 * pairs, 3 * channels, atoms), F32),
                pltpu.VMEM((atoms, pairs * atoms), BF16),
                pltpu.VMEM((atoms + ghosts, pairs * atoms), BF16),
                pltpu.VMEM((atoms + ghosts, pairs * atoms // 2), BF16),
                pltpu.VMEM((5 * pairs, channels, atoms), F32),
                pltpu.VMEM((5, 9, channels, atoms), F32),
                pltpu.VMEM((2, channels, pairs * atoms), BF16),
                pltpu.VMEM((3, 9, 8 * pairs, atoms), F32),
                pltpu.VMEM((3, atoms, pairs * atoms), BF16),
                pltpu.VMEM((ghosts, atoms), BF16),
                pltpu.VMEM((atoms, atoms), BF16),
                pltpu.VMEM((ghosts, atoms), BF16),
                pltpu.VMEM((atoms, ghosts), BF16),
                pltpu.VMEM((2 * hidden, 32), BF16),
                pltpu.VMEM((2, hidden, 3 * hidden), BF16),
                pltpu.VMEM((2, 3 * channels, 3 * hidden), BF16),
                pltpu.VMEM((channels, 9 * channels), BF16),
                pltpu.VMEM((3 * channels, 3 * channels), BF16),
                pltpu.VMEM((channels, atoms), F32),
                tuple(pltpu.VMEM((4, n, depth, channels), BF16) for n, depth in kinds),
                tuple(pltpu.VMEM((4, n, depth, channels), BF16) for n, depth in kinds),
                pltpu.SemaphoreType.DMA((4, len(kinds))),
                pltpu.SemaphoreType.DMA((4, len(kinds))),
                pltpu.VMEM((pairs, 2 * channels, atoms), F32),
                pltpu.VMEM((pairs // 2, 9, channels, atoms), F32),
                tuple(
                    (pltpu.SMEM if x is send_list else pltpu.VMEM)(x.shape, x.dtype)
                    for x in operands
                ),
                pltpu.SemaphoreType.DMA((len(operands),)),
            ],
            compiler_params=pltpu.CompilerParams(
                collective_id=0, has_side_effects=True, vmem_limit_bytes=56 * 1024 * 1024
            ),
        )(operands)
        site, forces = [pltpu.with_memory_space_constraint(x, pltpu.VMEM) for x in (site, forces)]
        return pl.pallas_call(
            finish,
            out_shape=(
                jax.ShapeDtypeStruct((atoms,), F32),
                jax.ShapeDtypeStruct((3, atoms), F32),
            ),
            in_specs=[vmem, vmem],
            out_specs=(vmem, vmem),
        )(site, forces)

    in_specs = (
        P(AXES),
        P("gx", "gy", "gz", None),
        P(None, AXES),
        P(None, None, AXES),
        P(),
        P(),
        P(),
        P(),
        P(),
        P(),
        P(),
        P(),
    )
    out_specs = (P(AXES), P(None, AXES))
    return jax.shard_map(body, mesh=mesh, in_specs=in_specs, out_specs=out_specs, check_vma=False)
```
